32 devices in a mesh: group: 2 (over y), tile: 16 (over z, x, core).
Axes of the slice: x: 2, y: 2, z: 4, core: 2. Of those that a mesh axis runs over, the one named last changes fastest.
Arguments:
- density: float32 [2, 2048, 1024], P(None, ('group', 'tile')), parts along dimension 1, may hold values from -6 to 6
- observed: float32 [6, 2048, 1024], P(None, ('group', 'tile')), parts along dimension 1, may hold values from -3 to 3
- active: int32 [2048, 1024], P(('group', 'tile')), parts along dimension 0, may hold values 0 or 1
- layer_depth: float32 [2], replicated, may hold values from 0.5 to 4
Outputs:
- predicted: float32 [6, 2048, 1024], P(None, ('group', 'tile')), parts along dimension 1
- gradient: float32 [2, 2048, 1024], P(None, ('group', 'tile')), parts along dimension 1
The draws below stay inside these ranges and needn't reach their ends.
There are 2 independent parts, one for each index of `group`. The reference program is written for one: setup_inputs(seed, part) draws one part's arguments, and reference() takes and returns one part's arrays. A program takes and returns all parts, laid end to end along the dimension named above; an argument that names none is the same for every part. Nothing has to cross between parts.
All inputs are finite; a program needn't handle non-finite values. No bound on the sum of `active` on one device may be relied on, other than what follows from the above.
Results may differ from the reference program's by a relative error of at most 0.0001.
Values sent between devices are 32-bit elements; how exact they have to be, the bound alone decides.
No kernel may reach another device: no remote copies, remote signals or barrier semaphores. Data moves between devices by JAX's collectives and lax.ppermute only.
A program may use at most 128 MiB of HBM per device.

```python
import math
import jax
import jax.numpy as jnp

NS = 1024
LAYERS = 2
COMPS = 6


def draw_layer_depth(key, part):
    key_depth = jax.random.fold_in(key, 11)
    key_shallow = jax.random.fold_in(key, 23)
    key_pick = jax.random.fold_in(key, 37)
    key_second = jax.random.fold_in(key, 41)
    spread = jax.random.uniform(key_depth, (LAYERS,), jnp.float32)
    depth = 0.5 * jnp.exp(spread * math.log(8.0))
    shallow = 0.5 + 0.25 * jax.random.uniform(key_shallow, (LAYERS,), jnp.float32)
    order = jax.random.permutation(key_pick, LAYERS)
    second = jax.random.randint(key_second, (), 0, 2)
    chosen = (order == 0) | (order == 1) & (second == 1)
    return jnp.where(chosen, shallow, depth).astype(jnp.float32)


def place_ends(result, own_key, smallest, largest):
    longest = result.shape.index(max(result.shape))
    spots = []
    for shift in (0, 1):
        where = [jax.random.randint(jax.random.fold_in(own_key, axis), (), 0, length) for axis, length in enumerate(result.shape)]
        where[longest] = (where[longest] + shift) % result.shape[longest]
        spots.append(tuple(where))
    return result.at[spots[0]].set(smallest).at[spots[1]].set(largest)


def block_levels(own_key, dims, shards, smallest, top_value):
    def one(axis_at, parts):
        steps = jax.random.uniform(jax.random.fold_in(jax.random.fold_in(own_key, 6), axis_at), (parts,), jnp.float32, smallest / len(shards), top_value / len(shards))
        return jnp.repeat(jnp.exp(steps), dims[axis_at] // parts).reshape((-1,) + (1,) * (len(dims) - axis_at - 1))

    loudness = one(*shards[0])
    for cut in shards[1:]:
        loudness = loudness * one(*cut)
    return loudness


def gaussian(key, extent, width, reach, pieces=(), kind=jnp.bfloat16):
    factor_of = block_levels(key, extent, pieces, -0.22, 0.18) if pieces else 1.0
    entries = jax.random.normal(key, extent, jnp.float32) * width * factor_of
    return jnp.minimum(jnp.maximum(entries, -reach), reach).astype(kind)


def setup_inputs(seed: int = 0, part: int = 0) -> dict:
    keys = jax.random.split(jax.random.key(seed), 5)
    part_splits = jax.random.split(jax.random.fold_in(keys[4], part), 5)
    density = gaussian(part_splits[0], (LAYERS, NS, NS), 1.0, 6.0, ((1, 16),), jnp.float32)
    observed = gaussian(part_splits[1], (COMPS, NS, NS), 0.5, 3.0, ((1, 16),), jnp.float32)
    active = place_ends((jax.random.randint(part_splits[2], (NS, NS), 0, 4) < 3).astype(jnp.int32), jax.random.fold_in(part_splits[2], 1), 0, 1)
    layer_depth = draw_layer_depth(jax.random.fold_in(keys[4], 71), part)
    return dict(density=density, observed=observed, active=active, layer_depth=layer_depth)


TWO_PI = 2.0 * math.pi

def signed_wave(index, period):
    signed = jnp.where(index < period // 2, index, index - period).astype(jnp.float32)
    return signed * (TWO_PI / period)

def multipliers(wave_x, wave_y, modulus):
    zeros = jnp.zeros_like(modulus)
    return [(-wave_x * wave_x, zeros), (-wave_x * wave_y, zeros), (zeros, wave_x * modulus), (-wave_y * wave_y, zeros), (zeros, wave_y * modulus), (modulus * modulus, zeros)]

def reference(density, observed, active, layer_depth):
    padded = 2 * NS
    index = jnp.arange(padded, dtype=jnp.int32)
    wave = signed_wave(index, padded)
    plane = jnp.ones((padded, padded), jnp.float32)
    wave_x = wave[:, None] * plane
    wave_y = wave[None, :] * plane
    nyquist = (index == padded // 2)[:, None] | (index == padded // 2)[None, :]
    modulus = jnp.sqrt(wave_x * wave_x + wave_y * wave_y)
    slab = jnp.where(modulus > 0, -jnp.expm1(-modulus) / jnp.maximum(modulus, 0.001), 1.0)
    active_cells = active.astype(jnp.float32)
    masked = density * active_cells[None]

    def layer_weight(layer):
        return jnp.where(nyquist, 0.0, jnp.exp(-modulus * layer_depth[layer]) * slab)
    summed = layer_weight(0) * jnp.fft.fft2(masked[0], s=(padded, padded))
    for layer in range(1, LAYERS):
        summed = summed + layer_weight(layer) * jnp.fft.fft2(masked[layer], s=(padded, padded))
    factors = multipliers(wave_x, wave_y, modulus)
    predicted = []
    for real_factor, imag_factor in factors:
        spectrum = summed * (real_factor + 1j * imag_factor)
        predicted.append(jnp.real(jnp.fft.ifft2(spectrum))[:NS, :NS])
    predicted = jnp.stack(predicted)
    residual = predicted - observed
    adjoint = None
    for comp in range(COMPS):
        real_factor, imag_factor = factors[comp]
        term = (real_factor - 1j * imag_factor) * jnp.fft.fft2(residual[comp], s=(padded, padded))
        adjoint = term if adjoint is None else adjoint + term
    gradient = []
    for layer in range(LAYERS):
        gradient.append(active_cells * jnp.real(jnp.fft.ifft2(layer_weight(layer) * adjoint))[:NS, :NS])
    return (predicted, jnp.stack(gradient))
```

```python
import functools
import math

import jax
import jax.numpy as jnp
import numpy as np
from jax import lax
from jax.experimental import pallas as pl
from jax.experimental.pallas import tpu as pltpu
from jax.sharding import PartitionSpec as P

LANES = 128
HIGH = lax.Precision.HIGH


def half_waves(side):
    groups = side // LANES
    step = 2 * groups
    even = np.arange(LANES // 2) * step
    rows = [np.concatenate([even, even + groups])]
    for g in range(1, groups):
        rows.append(np.arange(LANES) * step + g)
    index = np.stack(rows)
    return np.where(index < side, index, index - 2 * side)


def angle_parts(left, right, period):
    phase = (left[:, None].astype(np.int64) * right[None, :].astype(np.int64)) % period
    angle = phase * (2.0 * math.pi / period)
    return np.cos(angle), np.sin(angle)


def ring_order(chips):
    width = max(1, int(round(chips ** (1.0 / 3.0))))
    if chips % width:
        width = 1
    height = chips // width
    order = [z * width for z in range(height)]
    for z in reversed(range(height)):
        row = list(range(1, width))
        if (height - 1 - z) % 2:
            row.reverse()
        order += [z * width + x for x in row]
    return np.array(order)


def dot(a, b):
    return jnp.dot(a, b, precision=HIGH)


def halves(a):
    high = a.astype(jnp.bfloat16)
    return high, (a - high.astype(jnp.float32)).astype(jnp.bfloat16)


def np_halves(a):
    a = a.astype(np.float32)
    high = a.astype(jnp.bfloat16)
    return jnp.asarray(high), jnp.asarray((a - high.astype(np.float32)).astype(jnp.bfloat16))


def product(left, right, dims=((1,), (0,))):
    def one(a, b):
        return lax.dot_general(a, b, (dims, ((), ())), preferred_element_type=jnp.float32)

    return one(left[0], right[0]) + (one(left[0], right[1]) + one(left[1], right[0]))


def accumulate(terms):
    total = None
    for factor, value in terms:
        if abs(factor) < 1e-9:
            continue
        if abs(abs(factor) - 1.0) < 1e-9:
            if total is None:
                total = value if factor > 0 else -value
            else:
                total = total + value if factor > 0 else total - value
        else:
            scaled = value * np.float32(factor)
            total = scaled if total is None else total + scaled
    return total


def spread(f):
    count = len(f)
    half = count // 2
    plus = [f[a] + f[a + half] for a in range(half)]
    minus = [f[a] - f[a + half] for a in range(half)]
    even = [None] + [f[a] + f[count - a] for a in range(1, half)]
    odd = [None] + [f[a] - f[count - a] for a in range(1, half)]
    out = []
    for g in range(count):
        angle = [math.pi * a * g / count for a in range(count)]
        if g == 0:
            top = accumulate([(1.0, plus[a]) for a in range(0, half, 2)])
            low = accumulate([(1.0, plus[a]) for a in range(1, half, 2)])
            out.append((top + low, top - low))
        elif g % 2:
            p = accumulate([(1.0, f[0])] + [(math.cos(angle[a]), odd[a]) for a in range(1, half)])
            q = accumulate(
                [(math.sin(angle[half]), f[half])]
                + [(math.sin(angle[a]), even[a]) for a in range(1, half)]
            )
            out.append((p, q))
        else:
            base = minus if (g // 2) % 2 else plus
            p = accumulate([(math.cos(angle[a]), base[a]) for a in range(half)])
            q = accumulate([(math.sin(angle[a]), base[a]) for a in range(half)])
            out.append((p, q))
    return out


def gather(pairs):
    count = len(pairs)
    half = count // 2
    out = [None] * count

    def wave(a, g):
        angle = math.pi * a * g / count
        return [(math.cos(angle), pairs[g][0]), (math.sin(angle), pairs[g][1])]

    for a in range(half):
        same = [(1.0, pairs[0][0]), ((-1.0) ** a, pairs[0][1])]
        for g in range(4, count, 4):
            same += wave(a, g)
        flip = []
        for g in range(2, count, 4):
            flip += wave(a, g)
        same, flip = accumulate(same), accumulate(flip)
        out[a] = same + flip
        out[a + half] = same - flip
    odds = range(1, count, 2)
    for a in range(1, half):
        cosine = accumulate([(math.cos(math.pi * a * g / count), pairs[g][0]) for g in odds])
        sine = accumulate([(math.sin(math.pi * a * g / count), pairs[g][1]) for g in odds])
        out[a] = out[a] + (cosine + sine)
        out[count - a] = out[count - a] + (sine - cosine)
    out[0] = out[0] + accumulate([(1.0, pairs[g][0]) for g in odds])
    out[half] = out[half] + accumulate([(math.sin(math.pi * g / 2), pairs[g][1]) for g in odds])
    return out


def double(a):
    a = jnp.concatenate([a, a], axis=0)
    return jnp.concatenate([a, a], axis=1)


def turn(a, ky):
    return jnp.concatenate([-ky * a[:, LANES:], ky * a[:, :LANES]], axis=1)


def twofold(ky):
    return jnp.concatenate([ky, ky], axis=1)


STRIP = 16


def forward_kernel(
    spec, weight, modulus, wave, mix_h, mix_l, near_h, near_l, inv_h, inv_l,
    out, val_h, val_l, sum_h, sum_l, steep_h, steep_l,
):
    layers = spec.shape[0]
    groups = mix_h.shape[0]
    span = near_h.shape[0] // 3
    wide = 2 * LANES

    for l in range(layers):

        def strip(i, carry, l=l):
            at = pl.multiple_of(i * STRIP, STRIP)
            f = [spec[l, pl.ds(a * LANES + at, STRIP), :] for a in range(groups)]
            for g, (p, q) in enumerate(spread(f)):
                high, low = halves(p)
                val_h[l, g, pl.ds(at, STRIP), :] = high
                val_l[l, g, pl.ds(at, STRIP), :] = low
                high, low = halves(q)
                val_h[l, g, pl.ds(LANES + at, STRIP), :] = high
                val_l[l, g, pl.ds(LANES + at, STRIP), :] = low
            return carry

        lax.fori_loop(0, LANES // STRIP, strip, 0)

    for g in range(groups):
        total = None
        for l in range(layers):
            cols = product((mix_h[g], mix_l[g]), (val_h[l, g], val_l[l, g]))
            cols = cols * double(weight[l, g * LANES : (g + 1) * LANES, :])
            total = cols if total is None else total + cols
        here = pl.ds(g * wide, wide)
        sum_h[here, :], sum_l[here, :] = halves(total)
        steep = total * double(modulus[g * LANES : (g + 1) * LANES, :])
        steep_h[here, :], steep_l[here, :] = halves(steep)

    plain = product((near_h[...], near_l[...]), (sum_h[...], sum_l[...]))
    sloped = product(
        (near_h[: 2 * span], near_l[: 2 * span]), (steep_h[...], steep_l[...])
    )
    ky = wave[0, 0:1, :]
    both = twofold(ky)
    lines = jnp.concatenate(
        [
            plain[2 * span :],
            turn(plain[span : 2 * span], ky),
            sloped[span:],
            -(both * both) * plain[:span],
            turn(sloped[:span], ky),
        ]
    )
    part = product(halves(lines), (inv_h[...], inv_l[...]))

    @pl.when(pl.program_id(0) == 0)
    def _():
        out[...] = part

    @pl.when(pl.program_id(0) > 0)
    def _():
        out[...] += part


def adjoint_kernel(
    core, field, other, seen, weight, modulus, wave, mix_h, mix_l, far_h, far_l, inv_h, inv_l,
    predicted, grid_h, grid_l, rest_h, rest_l, val,
):
    layers = weight.shape[0]
    groups = mix_h.shape[0]
    span = seen.shape[1]
    rows = predicted.shape[1]
    wide = 2 * LANES

    @pl.when(pl.program_id(0) == 0)
    def _():
        def total(c, at, size):
            here = pl.ds(c * span + at, size)
            return field[here, :] + other[here, :]

        def strip(i, carry):
            at = pl.multiple_of(i * STRIP, STRIP)
            xx, xy, xz, yy, yz = [total(c, at, STRIP) for c in range(5)]
            zz = -(xx + yy)
            look = [seen[c, pl.ds(at, STRIP), :] for c in range(6)]
            rest_zz = zz - look[5]
            rest = [
                rest_zz - (yy - look[3]),
                xy - look[1],
                rest_zz - (xx - look[0]),
                yz - look[4],
                xz - look[2],
            ]
            for c, value in enumerate(rest):
                here = pl.ds(c * span + at, STRIP)
                rest_h[here, :], rest_l[here, :] = halves(value)
            return carry

        lax.fori_loop(0, span // STRIP, strip, 0)

        def own(i, carry):
            to = pl.multiple_of(i * 8, 8)
            at = pl.multiple_of(core[0] * rows + i * 8, 8)
            xx, xy, xz, yy, yz = [total(c, at, 8) for c in range(5)]
            for c, value in enumerate([xx, xy, xz, yy, yz, -(xx + yy)]):
                predicted[c, pl.ds(to, 8), :] = value
            return carry

        lax.fori_loop(0, rows // 8, own, 0)

    turned = ((1,), (1,))
    back = product((rest_h[...], rest_l[...]), (inv_h[...], inv_l[...]), turned)
    ky = wave[0, 0:1, :]
    both = twofold(ky)
    part = [back[c * span : (c + 1) * span] for c in range(5)]
    low = halves(jnp.concatenate([both * both * part[0], -turn(part[1], ky), -part[2]]))
    high = halves(jnp.concatenate([-turn(part[3], ky), part[4]]))

    for g in range(groups):
        here = pl.ds(g * wide, wide)
        sums = product((far_h[here, :], far_l[here, :]), low)
        slopes = product(
            (far_h[here, : 2 * span], far_l[here, : 2 * span]), high
        )
        sums = sums + double(modulus[g * LANES : (g + 1) * LANES, :]) * slopes
        for l in range(layers):
            scaled = sums * double(weight[l, g * LANES : (g + 1) * LANES, :])
            val[l, g] = product((mix_h[g], mix_l[g]), halves(scaled))

    for l in range(layers):

        def strip(i, carry, l=l):
            at = pl.multiple_of(i * STRIP, STRIP)
            pairs = [
                (val[l, g, pl.ds(at, STRIP), :], val[l, g, pl.ds(LANES + at, STRIP), :])
                for g in range(groups)
            ]
            for a, value in enumerate(gather(pairs)):
                here = pl.ds(a * LANES + at, STRIP)
                grid_h[l, here, :], grid_l[l, here, :] = halves(value)
            return carry

        lax.fori_loop(0, LANES // STRIP, strip, 0)


def body(density, observed, active, layer_depth):
    layers, rows, side = density.shape
    period = 2 * side
    tiles = lax.axis_size("tile")
    chips = tiles // 2
    place = lax.axis_index("tile")
    chip, core = place // 2, place % 2
    span = 2 * rows
    groups = side // LANES
    own = groups // 2
    wide = 2 * LANES

    order = ring_order(chips)
    spot = np.argsort(order)
    order_c = jnp.asarray(order, jnp.int32)
    pos = jnp.asarray(spot, jnp.int32)[chip]

    def ring(shift):
        return [
            (2 * int(order[p]) + c, 2 * int(order[(p + shift) % chips]) + c)
            for p in range(chips)
            for c in (0, 1)
        ]

    ahead, back = ring(1), ring(-1)
    pair = [(i, i ^ 1) for i in range(tiles)]

    def chip_at(offset):
        return order_c[lax.rem(pos + offset + 2 * chips, chips)]

    unit = 2.0 * math.pi / period
    waves = half_waves(side)
    cells = np.arange(side)
    cos_t, sin_t = angle_parts(cells, waves.reshape(-1), period)
    cos_t = cos_t.reshape(side, groups, 1, LANES)
    sin_t = sin_t.reshape(side, groups, 1, LANES)
    full_y = np.concatenate([cos_t, -sin_t], axis=2).reshape(side, 2, side).transpose(1, 0, 2)
    table_y = lax.dynamic_index_in_dim(jnp.asarray(full_y, jnp.float32), core, 0, False)
    inverse_y = [
        lax.dynamic_index_in_dim(a, core, 0, False) for a in np_halves(full_y.transpose(0, 2, 1))
    ]
    value = np.concatenate([cos_t, sin_t], axis=2).reshape(side, period)
    slope = np.concatenate([-sin_t, cos_t], axis=2).reshape(side, period)
    flat_wave = np.repeat((waves * unit)[:, None], 2, axis=1).reshape(1, period)
    near = np.stack([value, flat_wave * slope, -(flat_wave**2) * value])
    near = near.reshape(3, chips, span, period).transpose(1, 0, 2, 3).reshape(chips, 3 * span, period)
    near = [lax.dynamic_index_in_dim(a, chip, 0, False) for a in np_halves(near)]
    far = [a.T for a in near]

    low_cells = np.arange(LANES)
    mix = np.zeros((groups, 2 * LANES, 2 * LANES))
    for g in range(groups):
        c, s = angle_parts(waves[g], low_cells, period)
        if g:
            mix[g] = np.block([[c, -s], [s, c]])
        else:
            top = (np.arange(LANES) < LANES // 2)[:, None]
            mix[g] = np.block([[c * top, c * ~top], [s * top, s * ~top]])
    mix_f = np_halves(mix)
    mix_b = np_halves(mix.transpose(0, 2, 1))

    flat_x = jnp.asarray((waves * unit).reshape(-1, 1), jnp.float32)
    twice_x = jnp.asarray(np.where(waves == 0, 1.0, 2.0).reshape(-1, 1), jnp.float32)
    flat_y = lax.dynamic_slice_in_dim(flat_x, core * (side // 2), side // 2, 0).reshape(1, -1)
    twice_y = lax.dynamic_slice_in_dim(twice_x, core * (side // 2), side // 2, 0).reshape(1, -1)
    modulus = jnp.sqrt(flat_x * flat_x + flat_y * flat_y)
    slab = jnp.where(modulus > 0, -jnp.expm1(-modulus) / jnp.maximum(modulus, 0.001), 1.0)
    gain = slab * (twice_x * twice_y / (period * period))
    weight = jnp.exp(-modulus[None] * layer_depth[:, None, None]) * gain[None]
    wave = jnp.broadcast_to(flat_y.reshape(own, 1, LANES), (own, 8, LANES))

    active_cells = active.astype(jnp.float32)
    masked = density * active_cells[None]
    seen_other = lax.ppermute(observed, "tile", pair)
    seen = jnp.concatenate(
        [jnp.where(core == 0, observed, seen_other), jnp.where(core == 0, seen_other, observed)],
        axis=1,
    )

    if chips <= 8:
        spec = jnp.zeros((layers, side, side), jnp.float32)
        fore, rear = masked[0], masked[1]
        for step in range(chips):
            if step:
                fore = lax.ppermute(fore, "tile", ahead)
                rear = lax.ppermute(rear, "tile", back)
            both = jnp.stack([fore, rear])
            other = lax.ppermute(both, "tile", pair)
            first = jnp.where(core == 0, both, other)
            second = jnp.where(core == 0, other, both)
            block = jnp.concatenate([first, second], axis=1)
            out = dot(block.reshape(2 * span, side), table_y).reshape(2, span, side)
            spec = lax.dynamic_update_slice(spec, out[:1], (0, chip_at(-step) * span, 0))
            spec = lax.dynamic_update_slice(spec, out[1:], (1, chip_at(step) * span, 0))
    else:
        whole = lax.all_gather(masked, "tile", axis=1, tiled=True)
        spec = dot(whole.reshape(layers * side, side), table_y).reshape(layers, side, side)

    def const(shape):
        return pl.BlockSpec(shape, lambda g: (0,) * len(shape))

    def lanes(shape):
        return pl.BlockSpec(shape, lambda g: (0,) * (len(shape) - 1) + (g,))

    waves_spec = pl.BlockSpec((1, 8, LANES), lambda g: (g, 0, 0))
    inverse_spec = pl.BlockSpec((wide, side), lambda g: (g, 0))
    params = pltpu.CompilerParams(
        dimension_semantics=("arbitrary",), vmem_limit_bytes=56 * 1024 * 1024
    )
    partial = pl.pallas_call(
        forward_kernel,
        grid=(own,),
        in_specs=[
            lanes((layers, side, wide)),
            lanes((layers, side, LANES)),
            lanes((side, LANES)),
            waves_spec,
            const(mix.shape),
            const(mix.shape),
            const((3 * span, period)),
            const((3 * span, period)),
            inverse_spec,
            inverse_spec,
        ],
        out_specs=const((5 * span, side)),
        out_shape=jax.ShapeDtypeStruct((5 * span, side), jnp.float32),
        scratch_shapes=[
            pltpu.VMEM((layers, groups, wide, wide), jnp.bfloat16),
            pltpu.VMEM((layers, groups, wide, wide), jnp.bfloat16),
        ]
        + [pltpu.VMEM((period, wide), jnp.bfloat16)] * 4,
        compiler_params=params,
    )(spec, weight, modulus, wave, *mix_f, *near, *inverse_y)

    other = lax.ppermute(partial, "tile", pair)
    predicted, grid_h, grid_l = pl.pallas_call(
        adjoint_kernel,
        grid=(own,),
        in_specs=[
            pl.BlockSpec(memory_space=pltpu.SMEM),
            const((5 * span, side)),
            const((5 * span, side)),
            const((6, span, side)),
            lanes((layers, side, LANES)),
            lanes((side, LANES)),
            waves_spec,
            const(mix.shape),
            const(mix.shape),
            const((period, 3 * span)),
            const((period, 3 * span)),
            inverse_spec,
            inverse_spec,
        ],
        out_specs=[
            const((6, rows, side)),
            lanes((layers, side, wide)),
            lanes((layers, side, wide)),
        ],
        out_shape=[
            jax.ShapeDtypeStruct((6, rows, side), jnp.float32),
            jax.ShapeDtypeStruct((layers, side, side), jnp.bfloat16),
            jax.ShapeDtypeStruct((layers, side, side), jnp.bfloat16),
        ],
        scratch_shapes=[
            pltpu.VMEM((5 * span, side), jnp.bfloat16),
            pltpu.VMEM((5 * span, side), jnp.bfloat16),
            pltpu.VMEM((layers, groups, wide, wide), jnp.float32),
        ],
        compiler_params=params,
    )(
        core.reshape(1).astype(jnp.int32), partial, other, seen, weight, modulus, wave,
        *mix_b, *far, *inverse_y,
    )

    if chips <= 8:

        def share(grids, offset):
            strips = []
            for half in grids:
                strips.append(
                    jnp.concatenate(
                        [
                            lax.dynamic_slice(
                                half, (l, chip_at(o) * span, 0), (1, span, side)
                            )[0]
                            for l, o in ((0, -offset), (1, offset))
                        ]
                    )
                )
            strip = product(strips, inverse_y).reshape(2, span, side)
            keep = lax.dynamic_slice_in_dim(strip, core * rows, rows, 1)
            give = lax.dynamic_slice_in_dim(strip, (1 - core) * rows, rows, 1)
            return keep + lax.ppermute(give, "tile", pair)

        grids = (grid_h, grid_l)
        now = share(grids, 1)
        ready = share(grids, 2)
        for step in range(1, chips):
            fore = lax.ppermute(now[0], "tile", ahead)
            rear = lax.ppermute(now[1], "tile", back)
            if step < chips - 1:
                now, ready, grids = lax.optimization_barrier((now, ready, grids))
                later = share(grids, step + 2)
            now = ready + jnp.stack([fore, rear])
            if step < chips - 1:
                ready = later
        gradient = now
    else:
        strip = product(
            [a.reshape(layers * side, side) for a in (grid_h, grid_l)], inverse_y
        ).reshape(layers, side, side)
        gradient = lax.psum_scatter(strip, "tile", scatter_dimension=1, tiled=True)
    return (predicted, gradient * active_cells[None])


def solution(mesh):
    return jax.shard_map(
        body,
        mesh=mesh,
        in_specs=(
            P(None, ("group", "tile"), None),
            P(None, ("group", "tile"), None),
            P(("group", "tile"), None),
            P(),
        ),
        out_specs=(P(None, ("group", "tile"), None), P(None, ("group", "tile"), None)),
        check_vma=False,
    )
```

```python
import functools
import math

import jax
import jax.numpy as jnp
import numpy as np
from jax import lax
from jax.experimental import pallas as pl
from jax.experimental.pallas import tpu as pltpu
from jax.sharding import PartitionSpec as P

LANES = 128
HIGH = lax.Precision.HIGH


def half_waves(side):
    groups = side // LANES
    step = 2 * groups
    even = np.arange(LANES // 2) * step
    rows = [np.concatenate([even, even + groups])]
    for g in range(1, groups):
        rows.append(np.arange(LANES) * step + g)
    index = np.stack(rows)
    return np.where(index < side, index, index - 2 * side)


def angle_parts(left, right, period):
    phase = (left[:, None].astype(np.int64) * right[None, :].astype(np.int64)) % period
    angle = phase * (2.0 * math.pi / period)
    return np.cos(angle), np.sin(angle)


def ring_order(chips):
    width = max(1, int(round(chips ** (1.0 / 3.0))))
    if chips % width:
        width = 1
    height = chips // width
    order = [z * width for z in range(height)]
    for z in reversed(range(height)):
        row = list(range(1, width))
        if (height - 1 - z) % 2:
            row.reverse()
        order += [z * width + x for x in row]
    return np.array(order)


def dot(a, b):
    return jnp.dot(a, b, precision=HIGH)


def halves(a):
    high = a.astype(jnp.bfloat16)
    return high, (a - high.astype(jnp.float32)).astype(jnp.bfloat16)


def np_halves(a):
    a = a.astype(np.float32)
    high = a.astype(jnp.bfloat16)
    return high, (a - high.astype(np.float32)).astype(jnp.bfloat16)


def table_of(a, axis):
    return jnp.asarray(np.concatenate(np_halves(a), axis=axis))


def product(left, right, dims=((1,), (0,))):
    def one(a, b):
        return lax.dot_general(a, b, (dims, ((), ())), preferred_element_type=jnp.float32)

    return one(left[0], right[0]) + (one(left[0], right[1]) + one(left[1], right[0]))


def stacked(table, high, low, rows):
    both = jnp.dot(table, high, preferred_element_type=jnp.float32)
    rest = jnp.dot(table[:rows], low, preferred_element_type=jnp.float32)
    return both[:rows] + (both[rows:] + rest)


def mixed(values, high, low):
    rows = values.shape[0] // 2
    both = jnp.dot(values, high, preferred_element_type=jnp.float32)
    rest = jnp.dot(values[:rows], low, preferred_element_type=jnp.float32)
    return both[:rows] + (both[rows:] + rest)


def accumulate(terms):
    total = None
    for factor, value in terms:
        if abs(factor) < 1e-9:
            continue
        if abs(abs(factor) - 1.0) < 1e-9:
            if total is None:
                total = value if factor > 0 else -value
            else:
                total = total + value if factor > 0 else total - value
        else:
            scaled = value * np.float32(factor)
            total = scaled if total is None else total + scaled
    return total


def spread(f):
    count = len(f)
    half = count // 2
    plus = [f[a] + f[a + half] for a in range(half)]
    minus = [f[a] - f[a + half] for a in range(half)]
    even = [None] + [f[a] + f[count - a] for a in range(1, half)]
    odd = [None] + [f[a] - f[count - a] for a in range(1, half)]
    out = []
    for g in range(count):
        angle = [math.pi * a * g / count for a in range(count)]
        if g == 0:
            top = accumulate([(1.0, plus[a]) for a in range(0, half, 2)])
            low = accumulate([(1.0, plus[a]) for a in range(1, half, 2)])
            out.append((top + low, top - low))
        elif g % 2:
            p = accumulate([(1.0, f[0])] + [(math.cos(angle[a]), odd[a]) for a in range(1, half)])
            q = accumulate(
                [(math.sin(angle[half]), f[half])]
                + [(math.sin(angle[a]), even[a]) for a in range(1, half)]
            )
            out.append((p, q))
        else:
            base = minus if (g // 2) % 2 else plus
            p = accumulate([(math.cos(angle[a]), base[a]) for a in range(half)])
            q = accumulate([(math.sin(angle[a]), base[a]) for a in range(half)])
            out.append((p, q))
    return out


def gather(pairs):
    count = len(pairs)
    half = count // 2
    out = [None] * count
    there = [g for g in range(count) if pairs[g] is not None]

    def wave(a, g):
        angle = math.pi * a * g / count
        return [(math.cos(angle), pairs[g][0]), (math.sin(angle), pairs[g][1])]

    for a in range(half):
        same = []
        if 0 in there:
            same = [(1.0, pairs[0][0]), ((-1.0) ** a, pairs[0][1])]
        for g in there:
            if g and g % 4 == 0:
                same += wave(a, g)
        flip = []
        for g in there:
            if g % 4 == 2:
                flip += wave(a, g)
        same, flip = accumulate(same), accumulate(flip)
        out[a] = same + flip
        out[a + half] = same - flip
    odds = [g for g in there if g % 2]
    for a in range(1, half):
        cosine = accumulate([(math.cos(math.pi * a * g / count), pairs[g][0]) for g in odds])
        sine = accumulate([(math.sin(math.pi * a * g / count), pairs[g][1]) for g in odds])
        out[a] = out[a] + (cosine + sine)
        out[count - a] = out[count - a] + (sine - cosine)
    out[0] = out[0] + accumulate([(1.0, pairs[g][0]) for g in odds])
    out[half] = out[half] + accumulate([(math.sin(math.pi * g / 2), pairs[g][1]) for g in odds])
    return out


def double(a):
    a = jnp.concatenate([a, a], axis=0)
    return jnp.concatenate([a, a], axis=1)


def turn(a, ky):
    return jnp.concatenate([-ky * a[:, LANES:], ky * a[:, :LANES]], axis=1)


def twofold(ky):
    return jnp.concatenate([ky, ky], axis=1)


STRIP = 16


def decay(modulus, gain, depth, l, g):
    here = slice(g * LANES, (g + 1) * LANES)
    return jnp.exp(-modulus[0, here, :] * depth[l]) * gain[0, here, :]


def on_core(place, run):
    for c in (0, 1):

        @pl.when(place[0] == c)
        def _(c=c):
            run(c)


def split_lanes(core, own, read, write):
    sums = spread([read(slice(a * LANES, (a + 1) * LANES)) for a in range(2 * own)])
    for g in range(own):
        for k in (0, 1):
            write(g, slice(k * LANES, (k + 1) * LANES), *halves(sums[core * own + g][k]))


def join_lanes(core, own, read):
    pairs = [None] * (2 * own)
    for g in range(own):
        pairs[core * own + g] = (read(g, slice(0, LANES)), read(g, slice(LANES, 2 * LANES)))
    return gather(pairs)


def rows_kernel(later, place, fore, rear, far_fore, far_rear, mix_h, mix_l, *rest):
    spec_a, spec_b, val = rest[2:] if later else rest
    rows = fore.shape[0]
    own = mix_h.shape[1]
    span = 2 * rows
    wide = 2 * LANES

    def run(core):
        for l, pair in enumerate(((fore, far_fore), (rear, far_rear))):
            for k, source in enumerate(pair):
                start = l * span + (core if k == 0 else 1 - core) * rows
                for i in range(rows // STRIP):
                    at = slice(i * STRIP, (i + 1) * STRIP)
                    here = slice(start + i * STRIP, start + (i + 1) * STRIP)
                    below = slice(2 * span + here.start, 2 * span + here.stop)

                    def write(g, lane, high, low):
                        val[g, here, lane] = high
                        val[g, below, lane] = low

                    split_lanes(core, own, lambda lane: source[at, lane], write)

    on_core(place, run)
    for g in range(own):
        out = mixed(val[g], mix_h[0, g], mix_l[0, g])
        spec_a[:, g * wide : (g + 1) * wide] = out[:span]
        spec_b[:, g * wide : (g + 1) * wide] = out[span:]


def strips_kernel(place, high_a, low_a, high_b, low_b, mix_h, mix_l, keep, give, val):
    rows = keep.shape[1]
    own = mix_h.shape[1]
    span = 2 * rows
    for g in range(own):
        lanes = slice(g * 2 * LANES, (g + 1) * 2 * LANES)
        values = jnp.concatenate([a[:, lanes] for a in (high_a, high_b, low_a, low_b)])
        val[g] = mixed(values, mix_h[0, g], mix_l[0, g])

    def run(core):
        for l in (0, 1):
            for target, part in ((keep, core), (give, 1 - core)):
                for i in range(rows // 8):
                    start = l * span + part * rows + i * 8
                    blocks = join_lanes(
                        core, own, lambda g, lane: val[g, start : start + 8, lane]
                    )
                    for a, value in enumerate(blocks):
                        target[l, i * 8 : (i + 1) * 8, a * LANES : (a + 1) * LANES] = value

    on_core(place, run)


def forward_kernel(
    place, depth, spec_a, spec_b, gain, modulus, wave, mix, near, back_h, back_l,
    out, val_h, val_l, sum_h, sum_l, steep_h, steep_l, lines,
):
    specs = (spec_a, spec_b)
    layers = len(specs)
    groups = mix.shape[0]
    span = near.shape[1] // 6
    wide = 2 * LANES
    own = groups // 2

    for l in range(layers):

        def strip(i, carry, l=l):
            at = pl.multiple_of(i * STRIP, STRIP)
            f = [specs[l][pl.ds(a * LANES + at, STRIP), :] for a in range(groups)]
            for g, (p, q) in enumerate(spread(f)):
                high, low = halves(p)
                val_h[l, g, pl.ds(at, STRIP), :] = high
                val_l[l, g, pl.ds(at, STRIP), :] = low
                high, low = halves(q)
                val_h[l, g, pl.ds(LANES + at, STRIP), :] = high
                val_l[l, g, pl.ds(LANES + at, STRIP), :] = low
            return carry

        lax.fori_loop(0, LANES // STRIP, strip, 0)

    for g in range(groups):
        total = None
        for l in range(layers):
            cols = stacked(mix[g], val_h[l, g], val_l[l, g], wide)
            cols = cols * double(decay(modulus, gain, depth, l, g))
            total = cols if total is None else total + cols
        here = pl.ds(g * wide, wide)
        sum_h[here, :], sum_l[here, :] = halves(total)
        steep = total * double(modulus[0, g * LANES : (g + 1) * LANES, :])
        steep_h[here, :], steep_l[here, :] = halves(steep)

    plain = stacked(near[0], sum_h[...], sum_l[...], 3 * span)
    slopes = jnp.concatenate([near[0, : 2 * span], near[0, 3 * span : 5 * span]])
    sloped = stacked(slopes, steep_h[...], steep_l[...], 2 * span)
    ky = wave[0, 0, 0:1, :]
    both = twofold(ky)
    values = jnp.concatenate(
        [
            plain[2 * span :],
            turn(plain[span : 2 * span], ky),
            sloped[span:],
            -(both * both) * plain[:span],
            turn(sloped[:span], ky),
        ]
    )
    step = pl.program_id(0)
    lines[step] = mixed(jnp.concatenate(halves(values)), back_h[0, 0], back_l[0, 0])

    @pl.when(step == own - 1)
    def _():
        def run(core):
            def strip(i, carry):
                here = pl.ds(pl.multiple_of(i * 8, 8), 8)
                blocks = join_lanes(core, own, lambda g, lane: lines[g, here, lane])
                for a, value in enumerate(blocks):
                    out[here, a * LANES : (a + 1) * LANES] = value
                return carry

            lax.fori_loop(0, 5 * span // 8, strip, 0)

        on_core(place, run)


def transpose_kernel(place, near, far):
    for g in range(far.shape[0] // (2 * LANES)):
        lane = slice(g * 2 * LANES, (g + 1) * 2 * LANES)
        far[lane, :] = near[0, :, lane].T


def adjoint_kernel(
    place, depth, field, other, seen, far_seen, gain, modulus, wave, mix, far, fold_h, fold_l,
    predicted, high_a, low_a, high_b, low_b, left, val_y, val,
):
    grids = ((high_a, low_a), (high_b, low_b))
    layers = len(grids)
    groups = mix.shape[0]
    rows = predicted.shape[1]
    span = 2 * rows
    wide = 2 * LANES
    own = groups // 2

    @pl.when(pl.program_id(0) == 0)
    def _():
        def total(c, at):
            here = pl.ds(c * span + at, 8)
            return field[here, :] + other[here, :]

        def strip(start, look, write):
            def one(i, carry):
                to = pl.multiple_of(i * 8, 8)
                at = pl.multiple_of(start + i * 8, 8)
                xx, xy, xz, yy, yz = [total(c, at) for c in range(5)]
                zz = -(xx + yy)
                rest_zz = zz - look[5, pl.ds(to, 8), :]
                rest = [
                    rest_zz - (yy - look[3, pl.ds(to, 8), :]),
                    xy - look[1, pl.ds(to, 8), :],
                    rest_zz - (xx - look[0, pl.ds(to, 8), :]),
                    yz - look[4, pl.ds(to, 8), :],
                    xz - look[2, pl.ds(to, 8), :],
                ]
                for c, value in enumerate(rest):
                    left[pl.ds(c * span + at, 8), :] = value
                if write:
                    for c, value in enumerate([xx, xy, xz, yy, yz, zz]):
                        predicted[c, pl.ds(to, 8), :] = value
                return carry

            lax.fori_loop(0, rows // 8, one, 0)

        strip(place[0] * rows, seen, True)
        strip((1 - place[0]) * rows, far_seen, False)

        def run(core):
            def cut(i, carry):
                at = pl.multiple_of(i * STRIP, STRIP)
                here = pl.ds(at, STRIP)
                below = pl.ds(5 * span + at, STRIP)

                def write(g, lane, high, low):
                    val_y[g, here, lane] = high
                    val_y[g, below, lane] = low

                split_lanes(core, own, lambda lane: left[here, lane], write)
                return carry

            lax.fori_loop(0, 5 * span // STRIP, cut, 0)

        on_core(place, run)

    back = mixed(val_y[pl.program_id(0)], fold_h[0, 0], fold_l[0, 0])
    ky = wave[0, 0, 0:1, :]
    both = twofold(ky)
    part = [back[c * span : (c + 1) * span] for c in range(5)]
    low = halves(jnp.concatenate([both * both * part[0], -turn(part[1], ky), -part[2]]))
    high = halves(jnp.concatenate([-turn(part[3], ky), part[4]]))

    for g in range(groups):
        here = slice(g * wide, (g + 1) * wide)
        table = jnp.concatenate([far[here, : 3 * span], far[here, 3 * span :]])
        sums = stacked(table, *low, wide)
        slopes = stacked(table[:, : 2 * span], *high, wide)
        sums = sums + double(modulus[0, g * LANES : (g + 1) * LANES, :]) * slopes
        for l in range(layers):
            scaled = sums * double(decay(modulus, gain, depth, l, g))
            val[l, g] = stacked(mix[g], *halves(scaled), wide)

    for l in range(layers):

        def strip(i, carry, l=l):
            at = pl.multiple_of(i * STRIP, STRIP)
            pairs = [
                (val[l, g, pl.ds(at, STRIP), :], val[l, g, pl.ds(LANES + at, STRIP), :])
                for g in range(groups)
            ]
            for a, value in enumerate(gather(pairs)):
                here = pl.ds(a * LANES + at, STRIP)
                grids[l][0][here, :], grids[l][1][here, :] = halves(value)
            return carry

        lax.fori_loop(0, LANES // STRIP, strip, 0)


def body(density, observed, active, layer_depth):
    layers, rows, side = density.shape
    period = 2 * side
    tiles = lax.axis_size("tile")
    chips = tiles // 2
    place = lax.axis_index("tile")
    chip, core = place // 2, place % 2
    span = 2 * rows
    groups = side // LANES
    own = groups // 2
    wide = 2 * LANES

    order = ring_order(chips)
    spot = np.argsort(order)
    index = np.zeros((tiles, 2 + 2 * (chips + 1)), np.int32)
    for i in range(tiles):
        p = spot[i // 2]
        index[i, :2] = i % 2, i // 2
        for o in range(chips + 1):
            index[i, 2 + 2 * o] = order[(p - o) % chips]
            index[i, 3 + 2 * o] = order[(p + o) % chips]
    index = lax.dynamic_index_in_dim(jnp.asarray(index), place, 0, False)

    def ring(shift):
        return [
            (2 * int(order[p]) + c, 2 * int(order[(p + shift) % chips]) + c)
            for p in range(chips)
            for c in (0, 1)
        ]

    ahead, back = ring(1), ring(-1)
    pair = [(i, i ^ 1) for i in range(tiles)]

    unit = 2.0 * math.pi / period
    waves = half_waves(side)
    cells = np.arange(side)
    cos_t, sin_t = angle_parts(cells, waves.reshape(-1), period)
    cos_t = cos_t.reshape(side, groups, 1, LANES)
    sin_t = sin_t.reshape(side, groups, 1, LANES)
    full_y = np.concatenate([cos_t, -sin_t], axis=2).reshape(side, 2, side).transpose(1, 2, 0)
    value = np.concatenate([cos_t, sin_t], axis=2).reshape(side, period)
    slope = np.concatenate([-sin_t, cos_t], axis=2).reshape(side, period)
    flat_wave = np.repeat((waves * unit)[:, None], 2, axis=1).reshape(1, period)
    near = np.stack([value, flat_wave * slope, -(flat_wave**2) * value])
    near = near.reshape(3, chips, span, period).transpose(1, 0, 2, 3).reshape(chips, 3 * span, period)
    near = table_of(near, 1)

    low_cells = np.arange(LANES)
    mix = np.zeros((groups, 2 * LANES, 2 * LANES))
    for g in range(groups):
        c, s = angle_parts(waves[g], low_cells, period)
        if g:
            mix[g] = np.block([[c, -s], [s, c]])
        else:
            top = (np.arange(LANES) < LANES // 2)[:, None]
            mix[g] = np.block([[c * top, c * ~top], [s * top, s * ~top]])
    mix_f = table_of(mix, 1)
    mix_b = table_of(mix.transpose(0, 2, 1), 1)

    mix_y = mix.transpose(0, 2, 1) * np.repeat([1.0, -1.0], LANES)
    mix_y = mix_y.reshape(2, own, wide, wide)
    mix_yf = [jnp.asarray(a) for a in np_halves(mix_y)]
    mix_yb = [jnp.asarray(a) for a in np_halves(mix_y.transpose(0, 1, 3, 2))]

    flat_x = (waves * unit).reshape(1, -1, 1)
    flat_y = (waves * unit).reshape(2, 1, -1)
    modulus = np.sqrt(flat_x**2 + flat_y**2).astype(np.float32)
    slab = np.where(modulus > 0, -np.expm1(-modulus) / np.maximum(modulus, 0.001), 1.0)
    twice = np.where(waves == 0, 1.0, 2.0)
    gain = slab * (twice.reshape(1, -1, 1) * twice.reshape(2, 1, -1) / (period * period))
    modulus, gain = jnp.asarray(modulus), jnp.asarray(gain, jnp.float32)
    wave = np.broadcast_to((waves * unit).reshape(2, own, 1, LANES), (2, own, 8, LANES))
    wave = jnp.asarray(wave, jnp.float32)

    active_cells = active.astype(jnp.float32)
    masked = density * active_cells[None]
    far_seen = lax.ppermute(observed, "tile", pair)

    def const(shape):
        return pl.BlockSpec(shape, lambda g, *_: (0,) * len(shape))

    def lanes(shape):
        return pl.BlockSpec(shape, lambda g, *_: (0,) * (len(shape) - 1) + (g,))

    def by_core(shape):
        return pl.BlockSpec(shape, lambda g, p: (p[0],) + (0,) * (len(shape) - 1))

    def call(kernel, grid, in_specs, out_specs, out_shape, scratch, aliases={}):
        return pl.pallas_call(
            kernel,
            grid_spec=pltpu.PrefetchScalarGridSpec(
                num_scalar_prefetch=1,
                grid=(grid,),
                in_specs=in_specs,
                out_specs=out_specs,
                scratch_shapes=scratch,
            ),
            out_shape=out_shape,
            input_output_aliases=aliases,
            compiler_params=pltpu.CompilerParams(
                dimension_semantics=("arbitrary",), vmem_limit_bytes=56 * 1024 * 1024
            ),
        )

    def chip_block(shape, layer, offset):
        return pl.BlockSpec(shape, lambda g, p: (p[2 + 2 * offset + layer], 0))

    far = call(
        transpose_kernel,
        1,
        [pl.BlockSpec((1, 6 * span, period), lambda g, p: (p[1], 0, 0))],
        const((period, 6 * span)),
        jax.ShapeDtypeStruct((period, 6 * span), jnp.bfloat16),
        [],
    )(index, near)

    if chips <= 8:
        done = []
        fore, rear = masked[0], masked[1]
        for step in range(chips):
            if step:
                if step >= 2:
                    fore, rear, done[step - 2] = lax.optimization_barrier(
                        (fore, rear, done[step - 2])
                    )
                if step == 3:
                    fore, rear, far_seen, far = lax.optimization_barrier(
                        (fore, rear, far_seen, far)
                    )
                fore = lax.ppermute(fore, "tile", ahead)
                rear = lax.ppermute(rear, "tile", back)
            far_fore = lax.ppermute(fore, "tile", pair)
            far_rear = lax.ppermute(rear, "tile", pair)
            args = [index, fore, rear, far_fore, far_rear, *mix_yf]
            in_specs = [const((rows, side))] * 4 + [by_core((1,) + mix_y.shape[1:])] * 2
            if step:
                args += done[-1]
                in_specs += [pl.BlockSpec(memory_space=pl.ANY)] * 2
            spec = call(
                functools.partial(rows_kernel, step > 0),
                1,
                in_specs,
                [chip_block((span, side), l, step) for l in (0, 1)],
                [jax.ShapeDtypeStruct((side, side), jnp.float32)] * 2,
                [pltpu.VMEM((own, 4 * span, wide), jnp.bfloat16)],
                {7: 0, 8: 1} if step else {},
            )(*args)
            done.append(spec)
    else:
        whole = lax.all_gather(masked, "tile", axis=1, tiled=True)
        table_y = lax.dynamic_index_in_dim(jnp.asarray(full_y, jnp.float32), core, 0, False)
        spec = lax.dot_general(whole, table_y, (((2,), (1,)), ((), ())), precision=HIGH)
        spec = [spec[0], spec[1]]

    shared = [
        pl.BlockSpec((1, side, LANES), lambda g, p: (p[0], 0, g)),
        pl.BlockSpec((1, side, LANES), lambda g, p: (p[0], 0, g)),
        pl.BlockSpec((1, 1, 8, LANES), lambda g, p: (p[0], g, 0, 0)),
        const(mix_f.shape),
    ]
    group_spec = pl.BlockSpec((1, 1, wide, wide), lambda g, p: (p[0], g, 0, 0))
    smem = pl.BlockSpec(memory_space=pltpu.SMEM)
    partial = call(
        forward_kernel,
        own,
        [smem]
        + [lanes((side, wide))] * 2
        + shared
        + [pl.BlockSpec((1, 6 * span, period), lambda g, p: (p[1], 0, 0))]
        + [group_spec] * 2,
        const((5 * span, side)),
        jax.ShapeDtypeStruct((5 * span, side), jnp.float32),
        [pltpu.VMEM((layers, groups, wide, wide), jnp.bfloat16)] * 2
        + [pltpu.VMEM((period, wide), jnp.bfloat16)] * 4
        + [pltpu.VMEM((own, 5 * span, wide), jnp.float32)],
    )(index, layer_depth, *spec, gain, modulus, wave, mix_f, near, *mix_yb)

    other = lax.ppermute(partial, "tile", pair)
    predicted, *grids = call(
        adjoint_kernel,
        own,
        [smem]
        + [const((5 * span, side))] * 2
        + [const((6, rows, side))] * 2
        + shared
        + [const((period, 6 * span))]
        + [group_spec] * 2,
        [const((6, rows, side))] + [lanes((side, wide))] * 4,
        [jax.ShapeDtypeStruct((6, rows, side), jnp.float32)]
        + [jax.ShapeDtypeStruct((side, side), jnp.bfloat16)] * 4,
        [
            pltpu.VMEM((5 * span, side), jnp.float32),
            pltpu.VMEM((own, 10 * span, wide), jnp.bfloat16),
            pltpu.VMEM((layers, groups, wide, wide), jnp.float32),
        ],
    )(
        index, layer_depth, partial, other, observed, far_seen, gain, modulus, wave,
        mix_b, far, *mix_yf,
    )

    if chips <= 8:

        def share(offset, grids):
            keep, give = call(
                strips_kernel,
                1,
                [chip_block((span, side), l, offset) for l in (0, 0, 1, 1)]
                + [by_core((1,) + mix_y.shape[1:])] * 2,
                [const((layers, rows, side))] * 2,
                [jax.ShapeDtypeStruct((layers, rows, side), jnp.float32)] * 2,
                [pltpu.VMEM((own, 2 * span, wide), jnp.float32)],
            )(index, *grids, *mix_yb)
            return keep, lax.ppermute(give, "tile", pair)

        keep, give = share(1, grids)
        now = [keep[l] + give[l] for l in (0, 1)]
        ready = share(2, grids)
        for step in range(1, chips):
            keep, give = ready
            if step < chips - 1:
                now, grids = lax.optimization_barrier((now, grids))
                ready = share(step + 2, grids)
            fore = lax.ppermute(now[0], "tile", ahead)
            rear = lax.ppermute(now[1], "tile", back)
            now = [fore + (keep[0] + give[0]), rear + (keep[1] + give[1])]
        gradient = jnp.stack(now)
    else:
        table_y = lax.dynamic_index_in_dim(jnp.asarray(full_y, jnp.float32), core, 0, False)
        strip = jnp.stack([h.astype(jnp.float32) + l for h, l in (grids[:2], grids[2:])])
        strip = lax.dot_general(strip, table_y, (((2,), (0,)), ((), ())), precision=HIGH)
        gradient = lax.psum_scatter(strip, "tile", scatter_dimension=1, tiled=True)
    return (predicted, gradient * active_cells[None])


def solution(mesh):
    return jax.shard_map(
        body,
        mesh=mesh,
        in_specs=(
            P(None, ("group", "tile"), None),
            P(None, ("group", "tile"), None),
            P(("group", "tile"), None),
            P(),
        ),
        out_specs=(P(None, ("group", "tile"), None), P(None, ("group", "tile"), None)),
        check_vma=False,
    )
```

```python
import functools
import math

import jax
import jax.numpy as jnp
import numpy as np
from jax import lax
from jax.experimental import pallas as pl
from jax.experimental.pallas import tpu as pltpu
from jax.sharding import PartitionSpec as P

LANES = 128
HIGH = lax.Precision.HIGH


def half_waves(side):
    groups = side // LANES
    step = 2 * groups
    even = np.arange(LANES // 2) * step
    rows = [np.concatenate([even, even + groups])]
    for g in range(1, groups):
        rows.append(np.arange(LANES) * step + g)
    index = np.stack(rows)
    return np.where(index < side, index, index - 2 * side)


def angle_parts(left, right, period):
    phase = (left[:, None].astype(np.int64) * right[None, :].astype(np.int64)) % period
    angle = phase * (2.0 * math.pi / period)
    return np.cos(angle), np.sin(angle)


def ring_order(chips):
    width = max(1, int(round(chips ** (1.0 / 3.0))))
    if chips % width:
        width = 1
    height = chips // width
    order = [z * width for z in range(height)]
    for z in reversed(range(height)):
        row = list(range(1, width))
        if (height - 1 - z) % 2:
            row.reverse()
        order += [z * width + x for x in row]
    return np.array(order)


def dot(a, b):
    return jnp.dot(a, b, precision=HIGH)


def halves(a):
    high = a.astype(jnp.bfloat16)
    return high, (a - high.astype(jnp.float32)).astype(jnp.bfloat16)


def np_halves(a):
    a = a.astype(np.float32)
    high = a.astype(jnp.bfloat16)
    return high, (a - high.astype(np.float32)).astype(jnp.bfloat16)


def table_of(a, axis):
    return jnp.asarray(np.concatenate(np_halves(a), axis=axis))


def product(left, right, dims=((1,), (0,))):
    def one(a, b):
        return lax.dot_general(a, b, (dims, ((), ())), preferred_element_type=jnp.float32)

    return one(left[0], right[0]) + (one(left[0], right[1]) + one(left[1], right[0]))


def stacked(table, high, low, rows):
    both = jnp.dot(table, high, preferred_element_type=jnp.float32)
    rest = jnp.dot(table[:rows], low, preferred_element_type=jnp.float32)
    return both[:rows] + (both[rows:] + rest)


def mixed(values, high, low):
    rows = values.shape[0] // 2
    both = jnp.dot(values, high, preferred_element_type=jnp.float32)
    rest = jnp.dot(values[:rows], low, preferred_element_type=jnp.float32)
    return both[:rows] + (both[rows:] + rest)


def accumulate(terms):
    total = None
    for factor, value in terms:
        if abs(factor) < 1e-9:
            continue
        if abs(abs(factor) - 1.0) < 1e-9:
            if total is None:
                total = value if factor > 0 else -value
            else:
                total = total + value if factor > 0 else total - value
        else:
            scaled = value * np.float32(factor)
            total = scaled if total is None else total + scaled
    return total


def spread(f):
    count = len(f)
    half = count // 2
    plus = [f[a] + f[a + half] for a in range(half)]
    minus = [f[a] - f[a + half] for a in range(half)]
    even = [None] + [f[a] + f[count - a] for a in range(1, half)]
    odd = [None] + [f[a] - f[count - a] for a in range(1, half)]
    out = []
    for g in range(count):
        angle = [math.pi * a * g / count for a in range(count)]
        if g == 0:
            top = accumulate([(1.0, plus[a]) for a in range(0, half, 2)])
            low = accumulate([(1.0, plus[a]) for a in range(1, half, 2)])
            out.append((top + low, top - low))
        elif g % 2:
            p = accumulate([(1.0, f[0])] + [(math.cos(angle[a]), odd[a]) for a in range(1, half)])
            q = accumulate(
                [(math.sin(angle[half]), f[half])]
                + [(math.sin(angle[a]), even[a]) for a in range(1, half)]
            )
            out.append((p, q))
        else:
            base = minus if (g // 2) % 2 else plus
            p = accumulate([(math.cos(angle[a]), base[a]) for a in range(half)])
            q = accumulate([(math.sin(angle[a]), base[a]) for a in range(half)])
            out.append((p, q))
    return out


def gather(pairs):
    count = len(pairs)
    half = count // 2
    out = [None] * count
    there = [g for g in range(count) if pairs[g] is not None]

    def wave(a, g):
        angle = math.pi * a * g / count
        return [(math.cos(angle), pairs[g][0]), (math.sin(angle), pairs[g][1])]

    for a in range(half):
        same = []
        if 0 in there:
            same = [(1.0, pairs[0][0]), ((-1.0) ** a, pairs[0][1])]
        for g in there:
            if g and g % 4 == 0:
                same += wave(a, g)
        flip = []
        for g in there:
            if g % 4 == 2:
                flip += wave(a, g)
        same, flip = accumulate(same), accumulate(flip)
        out[a] = same + flip
        out[a + half] = same - flip
    odds = [g for g in there if g % 2]
    for a in range(1, half):
        cosine = accumulate([(math.cos(math.pi * a * g / count), pairs[g][0]) for g in odds])
        sine = accumulate([(math.sin(math.pi * a * g / count), pairs[g][1]) for g in odds])
        out[a] = out[a] + (cosine + sine)
        out[count - a] = out[count - a] + (sine - cosine)
    out[0] = out[0] + accumulate([(1.0, pairs[g][0]) for g in odds])
    out[half] = out[half] + accumulate([(math.sin(math.pi * g / 2), pairs[g][1]) for g in odds])
    return out


def double(a):
    a = jnp.concatenate([a, a], axis=0)
    return jnp.concatenate([a, a], axis=1)


def turn(a, ky):
    return jnp.concatenate([-ky * a[:, LANES:], ky * a[:, :LANES]], axis=1)


def twofold(ky):
    return jnp.concatenate([ky, ky], axis=1)


STRIP = 16


def length(wave_x, ky, g):
    kx = wave_x[g * LANES : (g + 1) * LANES, :]
    return jnp.sqrt(kx * kx + ky * ky)


def decay(modulus, gain, depth, l, g):
    return jnp.exp(-modulus * depth[l]) * gain[0, g * LANES : (g + 1) * LANES, :]


def on_core(place, run):
    for c in (0, 1):

        @pl.when(place[0] == c)
        def _(c=c):
            run(c)


def split_lanes(core, own, read, write):
    sums = spread([read(slice(a * LANES, (a + 1) * LANES)) for a in range(2 * own)])
    for g in range(own):
        for k in (0, 1):
            write(g, slice(k * LANES, (k + 1) * LANES), *halves(sums[core * own + g][k]))


def join_lanes(core, own, read):
    pairs = [None] * (2 * own)
    for g in range(own):
        pairs[core * own + g] = (read(g, slice(0, LANES)), read(g, slice(LANES, 2 * LANES)))
    return gather(pairs)


def rows_kernel(at, place, *refs):
    blocks, far, olds, spec, give, val = refs
    core = place[0]
    rows = (far[0][1] if give is None else give).shape[0] // 2
    span = 2 * rows

    def spot(offset, layer, whose):
        chip = place[2 + 2 * offset + layer]
        return pl.ds(pl.multiple_of(chip * span + whose * rows, rows), rows)

    for offset, source in far:
        for l in (0, 1):
            spec[l][spot(offset, l, 1 - core), :] = source[l * rows : (l + 1) * rows, :]
    if not blocks:
        return
    mix_h, mix_l = olds
    own = mix_h.shape[1]
    wide = 2 * LANES
    height = blocks[0].shape[0]
    for n, source in enumerate(blocks):
        for i in range(height // STRIP):
            strip = slice(i * STRIP, (i + 1) * STRIP)
            here = slice(n * height + strip.start, n * height + strip.stop)
            below = slice(span + here.start, span + here.stop)
            f = [source[strip, a * LANES : (a + 1) * LANES] for a in range(2 * own)]
            for g, pair in enumerate(spread(f)):
                for k, value in enumerate(pair):
                    lane = slice(k * LANES, (k + 1) * LANES)
                    val[g, here, lane], val[g, below, lane] = halves(value)
    for g in range(own):
        lane = slice(g * wide, (g + 1) * wide)
        out = mixed(val[core * own + g], mix_h[core, g], mix_l[core, g])
        for l in (0, 1):
            spec[l][spot(at, l, core), lane] = out[l * rows : (l + 1) * rows]
        peer = 1 - core
        give[:, lane] = mixed(val[peer * own + g], mix_h[peer, g], mix_l[peer, g])


def rows_first(place, a, b, mix_h, mix_l, spec_a, spec_b, give, val):
    rows_kernel(0, place, (a, b), (), (mix_h, mix_l), (spec_a, spec_b), give, val)


def rows_next(at, place, a, b, mix_h, mix_l, far, x, y, spec_a, spec_b, give, val):
    rows_kernel(at, place, (a, b), ((at - 1, far),), (mix_h, mix_l), (spec_a, spec_b), give, val)


def rows_apart(at, place, a, b, mix_h, mix_l, x, y, spec_a, spec_b, give, val):
    rows_kernel(at, place, (a, b), (), (mix_h, mix_l), (spec_a, spec_b), give, val)


def rows_last(at, place, before, far, x, y, spec_a, spec_b):
    rows_kernel(
        at, place, (), ((at - 1, before), (at, far)), None, (spec_a, spec_b), None, None
    )


def strips_kernel(at, place, high_a, low_a, high_b, low_b, mix_h, mix_l, *rest):
    keep, give, val = rest[:2], rest[2], rest[3]
    rows = keep[0].shape[0]
    own = mix_h.shape[1]
    span = 2 * rows
    spot = [pl.ds(pl.multiple_of(place[at + l] * span, span), span) for l in (0, 1)]
    for g in range(own):
        lanes = slice(g * 2 * LANES, (g + 1) * 2 * LANES)
        parts = ((high_a, 0), (high_b, 1), (low_a, 0), (low_b, 1))
        values = jnp.concatenate([a[spot[l], lanes] for a, l in parts])
        val[g] = mixed(values, mix_h[place[0], g], mix_l[place[0], g])

    def run(core):
        for l in (0, 1):
            for target, part, base in ((keep[l], core, 0), (give, 1 - core, l * rows)):
                for i in range(rows // 8):
                    start = l * span + part * rows + i * 8
                    blocks = join_lanes(
                        core, own, lambda g, lane: val[g, start : start + 8, lane]
                    )
                    here = slice(base + i * 8, base + (i + 1) * 8)
                    for a, value in enumerate(blocks):
                        target[here, a * LANES : (a + 1) * LANES] = value

    on_core(place, run)


def forward_kernel(
    place, depth, spec_a, spec_b, gain, wave_x, wave, mix, near, back_h, back_l,
    out, val_h, val_l, sum_h, sum_l, steep_h, steep_l, lines,
):
    specs = (spec_a, spec_b)
    layers = len(specs)
    groups = mix.shape[0]
    span = near.shape[0] // 6
    wide = 2 * LANES
    own = groups // 2
    step = pl.program_id(0)
    column = pl.ds(pl.multiple_of(step * wide, wide), wide)

    for l in range(layers):

        def strip(i, carry, l=l):
            at = pl.multiple_of(i * STRIP, STRIP)
            f = [specs[l][pl.ds(a * LANES + at, STRIP), column] for a in range(groups)]
            for g, (p, q) in enumerate(spread(f)):
                high, low = halves(p)
                val_h[l, g, pl.ds(at, STRIP), :] = high
                val_l[l, g, pl.ds(at, STRIP), :] = low
                high, low = halves(q)
                val_h[l, g, pl.ds(LANES + at, STRIP), :] = high
                val_l[l, g, pl.ds(LANES + at, STRIP), :] = low
            return carry

        lax.fori_loop(0, LANES // STRIP, strip, 0)

    ky = wave[0, 0, 0:1, :]
    for g in range(groups):
        total = None
        modulus = length(wave_x, ky, g)
        for l in range(layers):
            cols = stacked(mix[g], val_h[l, g], val_l[l, g], wide)
            cols = cols * double(decay(modulus, gain, depth, l, g))
            total = cols if total is None else total + cols
        here = pl.ds(g * wide, wide)
        sum_h[here, :], sum_l[here, :] = halves(total)
        steep = total * double(modulus)
        steep_h[here, :], steep_l[here, :] = halves(steep)

    plain = stacked(near[...], sum_h[...], sum_l[...], 3 * span)
    slopes = jnp.concatenate([near[: 2 * span], near[3 * span : 5 * span]])
    sloped = stacked(slopes, steep_h[...], steep_l[...], 2 * span)
    both = twofold(ky)
    values = jnp.concatenate(
        [
            plain[2 * span :],
            turn(plain[span : 2 * span], ky),
            sloped[span:],
            -(both * both) * plain[:span],
            turn(sloped[:span], ky),
        ]
    )
    lines[step] = mixed(jnp.concatenate(halves(values)), back_h[0, 0], back_l[0, 0])

    @pl.when(step == own - 1)
    def _():
        def run(core):
            def strip(i, carry):
                here = pl.ds(pl.multiple_of(i * 8, 8), 8)
                blocks = join_lanes(core, own, lambda g, lane: lines[g, here, lane])
                for a, value in enumerate(blocks):
                    out[here, a * LANES : (a + 1) * LANES] = value
                return carry

            lax.fori_loop(0, 5 * span // 8, strip, 0)

        on_core(place, run)


def near_kernel(place, base, rotate, wave, near, far):
    span = near.shape[0] // 6
    start = place[1] * span
    first = pl.multiple_of(lax.rem(start, LANES), STRIP)
    rows = pl.ds(first, span)
    block = lax.div(start, LANES)
    for g in range(far.shape[0]):
        lane = slice(g * LANES, (g + 1) * LANES)
        both = slice(2 * g * LANES, 2 * (g + 1) * LANES)
        cos_b, sin_b = base[0, rows, lane], base[1, rows, lane]
        cos_a, sin_a = rotate[block, 0:1, lane], rotate[block, 8:9, lane]
        c = cos_b * cos_a - sin_b * sin_a
        s = sin_b * cos_a + cos_b * sin_a
        k = wave[0:1, lane]
        value = jnp.concatenate([c, s], axis=1)
        slope = jnp.concatenate([-k * s, k * c], axis=1)
        bend = -twofold(k * k) * value
        for n, half in enumerate(halves(jnp.concatenate([value, slope, bend]))):
            near[n * 3 * span : (n + 1) * 3 * span, both] = half
            far[g, n * 2 * LANES : (n + 1) * 2 * LANES, :] = half.T


def adjoint_kernel(
    place, depth, field, other, seen, far_seen, gain, wave_x, wave, mix, far, fold_h, fold_l,
    predicted, high_a, low_a, high_b, low_b, left, val_y, val,
):
    grids = ((high_a, low_a), (high_b, low_b))
    layers = len(grids)
    groups = mix.shape[0]
    rows = predicted.shape[1]
    span = 2 * rows
    wide = 2 * LANES
    own = groups // 2

    @pl.when(pl.program_id(0) == 0)
    def _():
        def total(c, at):
            here = pl.ds(c * span + at, 8)
            return field[here, :] + other[here, :]

        def strip(start, look, write):
            def one(i, carry):
                to = pl.multiple_of(i * 8, 8)
                at = pl.multiple_of(start + i * 8, 8)
                xx, xy, xz, yy, yz = [total(c, at) for c in range(5)]
                zz = -(xx + yy)
                rest_zz = zz - look[5, pl.ds(to, 8), :]
                rest = [
                    rest_zz - (yy - look[3, pl.ds(to, 8), :]),
                    xy - look[1, pl.ds(to, 8), :],
                    rest_zz - (xx - look[0, pl.ds(to, 8), :]),
                    yz - look[4, pl.ds(to, 8), :],
                    xz - look[2, pl.ds(to, 8), :],
                ]
                for c, value in enumerate(rest):
                    left[pl.ds(c * span + at, 8), :] = value
                if write:
                    for c, value in enumerate([xx, xy, xz, yy, yz, zz]):
                        predicted[c, pl.ds(to, 8), :] = value
                return carry

            lax.fori_loop(0, rows // 8, one, 0)

        strip(place[0] * rows, seen, True)
        strip((1 - place[0]) * rows, far_seen, False)

        def run(core):
            def cut(i, carry):
                at = pl.multiple_of(i * STRIP, STRIP)
                here = pl.ds(at, STRIP)
                below = pl.ds(5 * span + at, STRIP)

                def write(g, lane, high, low):
                    val_y[g, here, lane] = high
                    val_y[g, below, lane] = low

                split_lanes(core, own, lambda lane: left[here, lane], write)
                return carry

            lax.fori_loop(0, 5 * span // STRIP, cut, 0)

        on_core(place, run)

    column = pl.ds(pl.multiple_of(pl.program_id(0) * wide, wide), wide)
    back = mixed(val_y[pl.program_id(0)], fold_h[0, 0], fold_l[0, 0])
    ky = wave[0, 0, 0:1, :]
    both = twofold(ky)
    part = [back[c * span : (c + 1) * span] for c in range(5)]
    low = halves(jnp.concatenate([both * both * part[0], -turn(part[1], ky), -part[2]]))
    high = halves(jnp.concatenate([-turn(part[3], ky), part[4]]))

    for g in range(groups):
        sums = stacked(far[g], *low, wide)
        slopes = stacked(far[g, :, : 2 * span], *high, wide)
        modulus = length(wave_x, ky, g)
        sums = sums + double(modulus) * slopes
        for l in range(layers):
            scaled = sums * double(decay(modulus, gain, depth, l, g))
            val[l, g] = stacked(mix[g], *halves(scaled), wide)

    for l in range(layers):

        def strip(i, carry, l=l):
            at = pl.multiple_of(i * STRIP, STRIP)
            pairs = [
                (val[l, g, pl.ds(at, STRIP), :], val[l, g, pl.ds(LANES + at, STRIP), :])
                for g in range(groups)
            ]
            for a, value in enumerate(gather(pairs)):
                here = pl.ds(a * LANES + at, STRIP)
                grids[l][0][here, column], grids[l][1][here, column] = halves(value)
            return carry

        lax.fori_loop(0, LANES // STRIP, strip, 0)


def body(density, observed, active, layer_depth):
    layers, rows, side = density.shape
    period = 2 * side
    tiles = lax.axis_size("tile")
    chips = tiles // 2
    place = lax.axis_index("tile")
    chip, core = place // 2, place % 2
    span = 2 * rows
    groups = side // LANES
    own = groups // 2
    wide = 2 * LANES

    order = ring_order(chips)
    spot = np.argsort(order)
    index = np.zeros((tiles, 2 + 2 * (chips + 1)), np.int32)
    for i in range(tiles):
        p = spot[i // 2]
        index[i, :2] = i % 2, i // 2
        for o in range(chips + 1):
            index[i, 2 + 2 * o] = order[(p - o) % chips]
            index[i, 3 + 2 * o] = order[(p + o) % chips]
    index = lax.dynamic_index_in_dim(jnp.asarray(index), place, 0, False)

    def ring(shift):
        return [
            (2 * int(order[p]) + c, 2 * int(order[(p + shift) % chips]) + c)
            for p in range(chips)
            for c in (0, 1)
        ]

    ahead, back = ring(1), ring(-1)
    pair = [(i, i ^ 1) for i in range(tiles)]

    unit = 2.0 * math.pi / period
    waves = half_waves(side)
    cells = np.arange(side)
    cos_t, sin_t = angle_parts(cells, waves.reshape(-1), period)
    cos_t = cos_t.reshape(side, groups, 1, LANES)
    sin_t = sin_t.reshape(side, groups, 1, LANES)
    full_y = np.concatenate([cos_t, -sin_t], axis=2).reshape(side, 2, side).transpose(1, 2, 0)
    base = np.stack(angle_parts(np.arange(LANES), waves.reshape(-1), period))
    base = jnp.asarray(base, jnp.float32)
    rotate = np.zeros((groups, 16, side))
    rotate[:, 0], rotate[:, 8] = angle_parts(np.arange(groups) * LANES, waves.reshape(-1), period)
    rotate = jnp.asarray(rotate, jnp.float32)
    line = jnp.asarray(np.broadcast_to((waves * unit).reshape(1, -1), (8, side)), jnp.float32)

    low_cells = np.arange(LANES)
    mix = np.zeros((groups, 2 * LANES, 2 * LANES))
    for g in range(groups):
        c, s = angle_parts(waves[g], low_cells, period)
        if g:
            mix[g] = np.block([[c, -s], [s, c]])
        else:
            top = (np.arange(LANES) < LANES // 2)[:, None]
            mix[g] = np.block([[c * top, c * ~top], [s * top, s * ~top]])
    mix_f = table_of(mix, 1)
    mix_b = table_of(mix.transpose(0, 2, 1), 1)

    mix_y = mix.transpose(0, 2, 1) * np.repeat([1.0, -1.0], LANES)
    mix_y = mix_y.reshape(2, own, wide, wide)
    mix_yf = [jnp.asarray(a) for a in np_halves(mix_y)]
    mix_yb = [jnp.asarray(a) for a in np_halves(mix_y.transpose(0, 1, 3, 2))]

    flat_x = (waves * unit).reshape(1, -1, 1)
    flat_y = (waves * unit).reshape(2, 1, -1)
    modulus = np.sqrt(flat_x**2 + flat_y**2).astype(np.float32)
    slab = np.where(modulus > 0, -np.expm1(-modulus) / np.maximum(modulus, 0.001), 1.0)
    twice = np.where(waves == 0, 1.0, 2.0)
    gain = slab * (twice.reshape(1, -1, 1) * twice.reshape(2, 1, -1) / (period * period))
    gain = jnp.asarray(gain, jnp.float32)
    wave_x = jnp.asarray(np.broadcast_to(flat_x[0], (side, LANES)), jnp.float32)
    wave = np.broadcast_to((waves * unit).reshape(2, own, 1, LANES), (2, own, 8, LANES))
    wave = jnp.asarray(wave, jnp.float32)

    far_seen = lax.ppermute(observed, "tile", pair)

    def const(shape):
        return pl.BlockSpec(shape, lambda g, *_: (0,) * len(shape))

    def lanes(shape):
        return pl.BlockSpec(shape, lambda g, *_: (0,) * (len(shape) - 1) + (g,))

    held = pl.BlockSpec(memory_space=pltpu.VMEM)

    def call(kernel, grid, in_specs, out_specs, out_shape, scratch, aliases={}, mib=20):
        return pl.pallas_call(
            kernel,
            grid_spec=pltpu.PrefetchScalarGridSpec(
                num_scalar_prefetch=1,
                grid=(grid,),
                in_specs=in_specs,
                out_specs=out_specs,
                scratch_shapes=scratch,
            ),
            out_shape=out_shape,
            input_output_aliases=aliases,
            compiler_params=pltpu.CompilerParams(
                dimension_semantics=("arbitrary",), vmem_limit_bytes=mib * 1024 * 1024
            ),
        )

    masked = density * active.astype(jnp.float32)[None]
    near, far = call(
        near_kernel,
        1,
        [held] * 3,
        [held] * 2,
        [
            jax.ShapeDtypeStruct((6 * span, period), jnp.bfloat16),
            jax.ShapeDtypeStruct((groups, 2 * wide, 3 * span), jnp.bfloat16),
        ],
        [],
        mib=4,
    )(index, base, rotate, line)

    if chips <= 8:
        chains = [masked[0], masked[1]]
        ways = (ahead, back)
        shapes = [jax.ShapeDtypeStruct((side, side), jnp.float32)] * 2
        shapes.append(jax.ShapeDtypeStruct((2 * rows, side), jnp.float32))

        def transformed(step, chains, far, spec):
            args = [index, *chains, *mix_yf]
            kernel, aliases = rows_first, {}
            if step:
                kernel = rows_apart if far is None else rows_next
                kernel = functools.partial(kernel, step)
                args += [*([] if far is None else [far]), *spec]
                aliases = {len(args) - 2: 0, len(args) - 1: 1}
            *spec, give = call(
                kernel,
                1,
                [held] * (len(args) - 1),
                [held] * 3,
                shapes,
                [pltpu.VMEM((groups, 2 * span, wide), jnp.bfloat16)],
                aliases,
                mib=4,
            )(*args)
            return spec, give

        spec = give = other = None
        for step in range(1, chips):
            if step >= 2:
                *chains, give = lax.optimization_barrier((*chains, give))
            came = [lax.ppermute(chains[l], "tile", ways[l]) for l in (0, 1)]
            if step >= 2:
                other = lax.ppermute(give, "tile", pair)
            if step == 4:
                other, near, far, far_seen = lax.optimization_barrier(
                    (other, near, far, far_seen)
                )
            spec, give = transformed(step - 1, chains, other, spec)
            chains = came
        other = lax.ppermute(give, "tile", pair)
        spec, give = transformed(chips - 1, chains, None, spec)
        spec = call(
            functools.partial(rows_last, chips - 1),
            1,
            [held] * 4,
            [held] * 2,
            shapes[:2],
            [],
            {3: 0, 4: 1},
            mib=4,
        )(index, other, lax.ppermute(give, "tile", pair), *spec)
    else:
        whole = lax.all_gather(masked, "tile", axis=1, tiled=True)
        table_y = lax.dynamic_index_in_dim(jnp.asarray(full_y, jnp.float32), core, 0, False)
        spec = lax.dot_general(whole, table_y, (((2,), (1,)), ((), ())), precision=HIGH)
        spec = [spec[0], spec[1]]

    shared = [
        pl.BlockSpec((1, side, LANES), lambda g, p: (p[0], 0, g)),
        held,
        pl.BlockSpec((1, 1, 8, LANES), lambda g, p: (p[0], g, 0, 0)),
        held,
    ]
    group_spec = pl.BlockSpec((1, 1, wide, wide), lambda g, p: (p[0], g, 0, 0))
    smem = pl.BlockSpec(memory_space=pltpu.SMEM)
    partial = call(
        forward_kernel,
        own,
        [smem]
        + [held] * 2
        + shared
        + [held]
        + [group_spec] * 2,
        held,
        jax.ShapeDtypeStruct((5 * span, side), jnp.float32),
        [pltpu.VMEM((layers, groups, wide, wide), jnp.bfloat16)] * 2
        + [pltpu.VMEM((period, wide), jnp.bfloat16)] * 4
        + [pltpu.VMEM((own, 5 * span, wide), jnp.float32)],
    )(index, layer_depth, *spec, gain, wave_x, wave, mix_f, near, *mix_yb)

    other = lax.ppermute(partial, "tile", pair)
    predicted, *grids = call(
        adjoint_kernel,
        own,
        [smem]
        + [held] * 4
        + shared
        + [held]
        + [group_spec] * 2,
        [const((6, rows, side))] + [held] * 4,
        [jax.ShapeDtypeStruct((6, rows, side), jnp.float32)]
        + [jax.ShapeDtypeStruct((side, side), jnp.bfloat16)] * 4,
        [
            pltpu.VMEM((5 * span, side), jnp.float32),
            pltpu.VMEM((own, 10 * span, wide), jnp.bfloat16),
            pltpu.VMEM((layers, groups, wide, wide), jnp.float32),
        ],
    )(
        index, layer_depth, partial, other, observed, far_seen, gain, wave_x, wave,
        mix_b, far, *mix_yf,
    )

    if chips <= 8:

        def share(offset, grids):
            out = call(
                functools.partial(strips_kernel, 2 + 2 * offset),
                1,
                [held] * 6,
                [held] * 3,
                [jax.ShapeDtypeStruct((rows, side), jnp.float32)] * 2
                + [jax.ShapeDtypeStruct((2 * rows, side), jnp.float32)],
                [pltpu.VMEM((own, 2 * span, wide), jnp.float32)],
                mib=4,
            )(index, *grids, *mix_yb)
            return out[:2], lax.ppermute(out[2], "tile", pair)

        def part(ready, l):
            keep, give = ready
            return keep[l] + give[l * rows : (l + 1) * rows]

        ready = share(1, grids)
        now = [part(ready, l) for l in (0, 1)]
        ready = share(2, grids)
        for step in range(1, chips):
            current = ready
            if step < chips - 1:
                now[1], grids = lax.optimization_barrier((now[1], grids))
                ready = share(step + 2, grids)
            now = [lax.ppermute(now[l], "tile", ways[l]) + part(current, l) for l in (0, 1)]
        gradient = jnp.stack(now)
    else:
        table_y = lax.dynamic_index_in_dim(jnp.asarray(full_y, jnp.float32), core, 0, False)
        strip = jnp.stack([h.astype(jnp.float32) + l for h, l in (grids[:2], grids[2:])])
        strip = lax.dot_general(strip, table_y, (((2,), (0,)), ((), ())), precision=HIGH)
        gradient = lax.psum_scatter(strip, "tile", scatter_dimension=1, tiled=True)
    return (predicted, gradient * active.astype(jnp.float32)[None])


def solution(mesh):
    return jax.shard_map(
        body,
        mesh=mesh,
        in_specs=(
            P(None, ("group", "tile"), None),
            P(None, ("group", "tile"), None),
            P(("group", "tile"), None),
            P(),
        ),
        out_specs=(P(None, ("group", "tile"), None), P(None, ("group", "tile"), None)),
        check_vma=False,
    )
```

```python
import functools
import math

import jax
import jax.numpy as jnp
import numpy as np
from jax import lax
from jax.experimental import pallas as pl
from jax.experimental.pallas import tpu as pltpu
from jax.sharding import PartitionSpec as P

LANES = 128
HIGH = lax.Precision.HIGH


def half_waves(side):
    groups = side // LANES
    step = 2 * groups
    even = np.arange(LANES // 2) * step
    rows = [np.concatenate([even, even + groups])]
    for g in range(1, groups):
        rows.append(np.arange(LANES) * step + g)
    index = np.stack(rows)
    return np.where(index < side, index, index - 2 * side)


def angle_parts(left, right, period):
    phase = (left[:, None].astype(np.int64) * right[None, :].astype(np.int64)) % period
    angle = phase * (2.0 * math.pi / period)
    return np.cos(angle), np.sin(angle)


def ring_order(chips):
    width = max(1, int(round(chips ** (1.0 / 3.0))))
    if chips % width:
        width = 1
    height = chips // width
    order = [z * width for z in range(height)]
    for z in reversed(range(height)):
        row = list(range(1, width))
        if (height - 1 - z) % 2:
            row.reverse()
        order += [z * width + x for x in row]
    return np.array(order)


def dot(a, b):
    return jnp.dot(a, b, precision=HIGH)


def halves(a):
    high = a.astype(jnp.bfloat16)
    return high, (a - high.astype(jnp.float32)).astype(jnp.bfloat16)


def np_halves(a):
    a = a.astype(np.float32)
    high = a.astype(jnp.bfloat16)
    return high, (a - high.astype(np.float32)).astype(jnp.bfloat16)


def table_of(a, axis):
    return jnp.asarray(np.concatenate(np_halves(a), axis=axis))


def product(left, right, dims=((1,), (0,))):
    def one(a, b):
        return lax.dot_general(a, b, (dims, ((), ())), preferred_element_type=jnp.float32)

    return one(left[0], right[0]) + (one(left[0], right[1]) + one(left[1], right[0]))


def stacked(table, high, low, rows):
    both = jnp.dot(table, high, preferred_element_type=jnp.float32)
    rest = jnp.dot(table[:rows], low, preferred_element_type=jnp.float32)
    return both[:rows] + (both[rows:] + rest)


def mixed(values, high, low):
    rows = values.shape[0] // 2
    both = jnp.dot(values, high, preferred_element_type=jnp.float32)
    rest = jnp.dot(values[:rows], low, preferred_element_type=jnp.float32)
    return both[:rows] + (both[rows:] + rest)


def accumulate(terms):
    total = None
    for factor, value in terms:
        if abs(factor) < 1e-9:
            continue
        if abs(abs(factor) - 1.0) < 1e-9:
            if total is None:
                total = value if factor > 0 else -value
            else:
                total = total + value if factor > 0 else total - value
        else:
            scaled = value * np.float32(factor)
            total = scaled if total is None else total + scaled
    return total


def spread(f):
    count = len(f)
    half = count // 2
    plus = [f[a] + f[a + half] for a in range(half)]
    minus = [f[a] - f[a + half] for a in range(half)]
    even = [None] + [f[a] + f[count - a] for a in range(1, half)]
    odd = [None] + [f[a] - f[count - a] for a in range(1, half)]
    out = []
    for g in range(count):
        angle = [math.pi * a * g / count for a in range(count)]
        if g == 0:
            top = accumulate([(1.0, plus[a]) for a in range(0, half, 2)])
            low = accumulate([(1.0, plus[a]) for a in range(1, half, 2)])
            out.append((top + low, top - low))
        elif g % 2:
            p = accumulate([(1.0, f[0])] + [(math.cos(angle[a]), odd[a]) for a in range(1, half)])
            q = accumulate(
                [(math.sin(angle[half]), f[half])]
                + [(math.sin(angle[a]), even[a]) for a in range(1, half)]
            )
            out.append((p, q))
        else:
            base = minus if (g // 2) % 2 else plus
            p = accumulate([(math.cos(angle[a]), base[a]) for a in range(half)])
            q = accumulate([(math.sin(angle[a]), base[a]) for a in range(half)])
            out.append((p, q))
    return out


def gather(pairs):
    count = len(pairs)
    half = count // 2
    out = [None] * count
    there = [g for g in range(count) if pairs[g] is not None]

    def wave(a, g):
        angle = math.pi * a * g / count
        return [(math.cos(angle), pairs[g][0]), (math.sin(angle), pairs[g][1])]

    for a in range(half):
        same = []
        if 0 in there:
            same = [(1.0, pairs[0][0]), ((-1.0) ** a, pairs[0][1])]
        for g in there:
            if g and g % 4 == 0:
                same += wave(a, g)
        flip = []
        for g in there:
            if g % 4 == 2:
                flip += wave(a, g)
        same, flip = accumulate(same), accumulate(flip)
        out[a] = same + flip
        out[a + half] = same - flip
    odds = [g for g in there if g % 2]
    for a in range(1, half):
        cosine = accumulate([(math.cos(math.pi * a * g / count), pairs[g][0]) for g in odds])
        sine = accumulate([(math.sin(math.pi * a * g / count), pairs[g][1]) for g in odds])
        out[a] = out[a] + (cosine + sine)
        out[count - a] = out[count - a] + (sine - cosine)
    out[0] = out[0] + accumulate([(1.0, pairs[g][0]) for g in odds])
    out[half] = out[half] + accumulate([(math.sin(math.pi * g / 2), pairs[g][1]) for g in odds])
    return out


def double(a):
    a = jnp.concatenate([a, a], axis=0)
    return jnp.concatenate([a, a], axis=1)


def turn(a, ky):
    return jnp.concatenate([-ky * a[:, LANES:], ky * a[:, :LANES]], axis=1)


def twofold(ky):
    return jnp.concatenate([ky, ky], axis=1)


STRIP = 16


def length(wave_x, ky, g):
    kx = wave_x[g * LANES : (g + 1) * LANES, :]
    return jnp.sqrt(kx * kx + ky * ky)


def decay(modulus, gain, depth, l, g):
    lane = pl.ds(pl.multiple_of(pl.program_id(0) * LANES, LANES), LANES)
    return jnp.exp(-modulus * depth[l]) * gain[g * LANES : (g + 1) * LANES, lane]


def on_core(place, run):
    for c in (0, 1):

        @pl.when(place[0] == c)
        def _(c=c):
            run(c)


def split_lanes(core, own, read, write):
    sums = spread([read(slice(a * LANES, (a + 1) * LANES)) for a in range(2 * own)])
    for g in range(own):
        for k in (0, 1):
            write(g, slice(k * LANES, (k + 1) * LANES), *halves(sums[core * own + g][k]))


def join_lanes(core, own, read):
    pairs = [None] * (2 * own)
    for g in range(own):
        pairs[core * own + g] = (read(g, slice(0, LANES)), read(g, slice(LANES, 2 * LANES)))
    return gather(pairs)


def rows_kernel(at, place, *refs):
    blocks, far, olds, spec, give, val = refs
    core = place[0]
    rows = (far[0][1] if give is None else give).shape[0] // 2
    span = 2 * rows

    def spot(offset, layer, whose):
        chip = place[2 + 2 * offset + layer]
        return pl.ds(pl.multiple_of(chip * span + whose * rows, rows), rows)

    for offset, source in far:
        for l in (0, 1):
            spec[l][spot(offset, l, 1 - core), :] = source[l * rows : (l + 1) * rows, :]
    if not blocks:
        return
    mix_h, mix_l = olds
    own = mix_h.shape[1]
    wide = 2 * LANES
    height = blocks[0].shape[0]
    for n, source in enumerate(blocks):
        for i in range(height // STRIP):
            strip = slice(i * STRIP, (i + 1) * STRIP)
            here = slice(n * height + strip.start, n * height + strip.stop)
            below = slice(span + here.start, span + here.stop)
            f = [source[strip, a * LANES : (a + 1) * LANES] for a in range(2 * own)]
            for g, pair in enumerate(spread(f)):
                for k, value in enumerate(pair):
                    lane = slice(k * LANES, (k + 1) * LANES)
                    val[g, here, lane], val[g, below, lane] = halves(value)
    for g in range(own):
        lane = slice(g * wide, (g + 1) * wide)
        out = mixed(val[core * own + g], mix_h[core, g], mix_l[core, g])
        for l in (0, 1):
            spec[l][spot(at, l, core), lane] = out[l * rows : (l + 1) * rows]
        peer = 1 - core
        give[:, lane] = mixed(val[peer * own + g], mix_h[peer, g], mix_l[peer, g])


def rows_first(place, a, b, mix_h, mix_l, spec_a, spec_b, give, val):
    rows_kernel(0, place, (a, b), (), (mix_h, mix_l), (spec_a, spec_b), give, val)


def rows_next(at, place, a, b, mix_h, mix_l, far, x, y, spec_a, spec_b, give, val):
    rows_kernel(at, place, (a, b), ((at - 1, far),), (mix_h, mix_l), (spec_a, spec_b), give, val)


def rows_apart(at, place, a, b, mix_h, mix_l, x, y, spec_a, spec_b, give, val):
    rows_kernel(at, place, (a, b), (), (mix_h, mix_l), (spec_a, spec_b), give, val)


def rows_last(at, place, before, far, x, y, spec_a, spec_b):
    rows_kernel(
        at, place, (), ((at - 1, before), (at, far)), None, (spec_a, spec_b), None, None
    )


def strips_kernel(at, place, high_a, low_a, high_b, low_b, mix_h, mix_l, *rest):
    keep, give, val = rest[:2], rest[2], rest[3]
    rows = keep[0].shape[0]
    own = mix_h.shape[1]
    span = 2 * rows
    spot = [pl.ds(pl.multiple_of(place[at + l] * span, span), span) for l in (0, 1)]
    for g in range(own):
        lanes = slice(g * 2 * LANES, (g + 1) * 2 * LANES)
        parts = ((high_a, 0), (high_b, 1), (low_a, 0), (low_b, 1))
        values = jnp.concatenate([a[spot[l], lanes] for a, l in parts])
        val[g] = mixed(values, mix_h[place[0], g], mix_l[place[0], g])

    def run(core):
        for l in (0, 1):
            for target, part, base in ((keep[l], core, 0), (give, 1 - core, l * rows)):
                for i in range(rows // 8):
                    start = l * span + part * rows + i * 8
                    blocks = join_lanes(
                        core, own, lambda g, lane: val[g, start : start + 8, lane]
                    )
                    here = slice(base + i * 8, base + (i + 1) * 8)
                    for a, value in enumerate(blocks):
                        target[here, a * LANES : (a + 1) * LANES] = value

    on_core(place, run)


def forward_kernel(
    place, depth, spec_a, spec_b, gain, wave_x, wave, mix, near, back_h, back_l,
    out, val_h, val_l, sum_h, sum_l, steep_h, steep_l, lines,
):
    specs = (spec_a, spec_b)
    layers = len(specs)
    groups = mix.shape[0]
    span = near.shape[0] // 6
    wide = 2 * LANES
    own = groups // 2
    step = pl.program_id(0)
    column = pl.ds(pl.multiple_of(step * wide, wide), wide)

    for l in range(layers):

        def strip(i, carry, l=l):
            at = pl.multiple_of(i * STRIP, STRIP)
            f = [specs[l][pl.ds(a * LANES + at, STRIP), column] for a in range(groups)]
            for g, (p, q) in enumerate(spread(f)):
                high, low = halves(p)
                val_h[l, g, pl.ds(at, STRIP), :] = high
                val_l[l, g, pl.ds(at, STRIP), :] = low
                high, low = halves(q)
                val_h[l, g, pl.ds(LANES + at, STRIP), :] = high
                val_l[l, g, pl.ds(LANES + at, STRIP), :] = low
            return carry

        lax.fori_loop(0, LANES // STRIP, strip, 0, unroll=True)

    ky = wave[0, 0, 0:1, :]
    for g in range(groups):
        total = None
        modulus = length(wave_x, ky, g)
        for l in range(layers):
            cols = stacked(mix[g], val_h[l, g], val_l[l, g], wide)
            cols = cols * double(decay(modulus, gain, depth, l, g))
            total = cols if total is None else total + cols
        here = pl.ds(g * wide, wide)
        sum_h[here, :], sum_l[here, :] = halves(total)
        steep = total * double(modulus)
        steep_h[here, :], steep_l[here, :] = halves(steep)

    plain = stacked(near[...], sum_h[...], sum_l[...], 3 * span)
    slopes = jnp.concatenate([near[: 2 * span], near[3 * span : 5 * span]])
    sloped = stacked(slopes, steep_h[...], steep_l[...], 2 * span)
    both = twofold(ky)
    values = jnp.concatenate(
        [
            plain[2 * span :],
            turn(plain[span : 2 * span], ky),
            sloped[span:],
            -(both * both) * plain[:span],
            turn(sloped[:span], ky),
        ]
    )
    lines[step] = mixed(jnp.concatenate(halves(values)), back_h[0, 0], back_l[0, 0])

    @pl.when(step == own - 1)
    def _():
        def run(core):
            def strip(i, carry):
                here = pl.ds(pl.multiple_of(i * 8, 8), 8)
                blocks = join_lanes(core, own, lambda g, lane: lines[g, here, lane])
                for a, value in enumerate(blocks):
                    out[here, a * LANES : (a + 1) * LANES] = value
                return carry

            lax.fori_loop(0, 5 * span // 8, strip, 0)

        on_core(place, run)


def near_kernel(place, base, rotate, wave, gains, near, far, gain):
    span = near.shape[0] // 6
    start = place[1] * span
    first = pl.multiple_of(lax.rem(start, LANES), STRIP)
    rows = pl.ds(first, span)
    block = lax.div(start, LANES)
    groups = rotate.shape[0]
    gain[...] = gains[place[0]]
    for g in range(groups):
        lane = slice(g * LANES, (g + 1) * LANES)
        both = slice(2 * g * LANES, 2 * (g + 1) * LANES)
        cos_b, sin_b = base[0, rows, lane], base[1, rows, lane]
        cos_a, sin_a = rotate[block, 0:1, lane], rotate[block, 8:9, lane]
        c = cos_b * cos_a - sin_b * sin_a
        s = sin_b * cos_a + cos_b * sin_a
        k = wave[0:1, lane]
        value = jnp.concatenate([c, s], axis=1)
        slope = jnp.concatenate([-k * s, k * c], axis=1)
        bend = -twofold(k * k) * value
        for n, half in enumerate(halves(jnp.concatenate([value, slope, bend]))):
            near[n * 3 * span : (n + 1) * 3 * span, both] = half
            far[pl.ds((n * groups + g) * 2 * LANES, 2 * LANES), :] = half.T


def adjoint_kernel(
    place, depth, field, other, seen, far_seen, gain, wave_x, wave, mix, far, fold_h, fold_l,
    predicted, high_a, low_a, high_b, low_b, left, val_y, val, sums_all, slopes_all,
):
    grids = ((high_a, low_a), (high_b, low_b))
    layers = len(grids)
    groups = mix.shape[0]
    rows = predicted.shape[1]
    span = 2 * rows
    wide = 2 * LANES
    own = groups // 2

    @pl.when(pl.program_id(0) == 0)
    def _():
        def total(c, at):
            here = pl.ds(c * span + at, 8)
            return field[here, :] + other[here, :]

        def strip(start, look, write):
            def one(i, carry):
                to = pl.multiple_of(i * 8, 8)
                at = pl.multiple_of(start + i * 8, 8)
                xx, xy, xz, yy, yz = [total(c, at) for c in range(5)]
                zz = -(xx + yy)
                rest_zz = zz - look[5, pl.ds(to, 8), :]
                rest = [
                    rest_zz - (yy - look[3, pl.ds(to, 8), :]),
                    xy - look[1, pl.ds(to, 8), :],
                    rest_zz - (xx - look[0, pl.ds(to, 8), :]),
                    yz - look[4, pl.ds(to, 8), :],
                    xz - look[2, pl.ds(to, 8), :],
                ]
                for c, value in enumerate(rest):
                    left[pl.ds(c * span + at, 8), :] = value
                if write:
                    for c, value in enumerate([xx, xy, xz, yy, yz, zz]):
                        predicted[c, pl.ds(to, 8), :] = value
                return carry

            lax.fori_loop(0, rows // 8, one, 0)

        strip(place[0] * rows, seen, True)
        strip((1 - place[0]) * rows, far_seen, False)

        def run(core):
            def cut(i, carry):
                at = pl.multiple_of(i * STRIP, STRIP)
                here = pl.ds(at, STRIP)
                below = pl.ds(5 * span + at, STRIP)

                def write(g, lane, high, low):
                    val_y[g, here, lane] = high
                    val_y[g, below, lane] = low

                split_lanes(core, own, lambda lane: left[here, lane], write)
                return carry

            lax.fori_loop(0, 5 * span // STRIP, cut, 0)

        on_core(place, run)

    column = pl.ds(pl.multiple_of(pl.program_id(0) * wide, wide), wide)
    back = mixed(val_y[pl.program_id(0)], fold_h[0, 0], fold_l[0, 0])
    ky = wave[0, 0, 0:1, :]
    both = twofold(ky)
    part = [back[c * span : (c + 1) * span] for c in range(5)]
    low = halves(jnp.concatenate([both * both * part[0], -turn(part[1], ky), -part[2]]))
    high = halves(jnp.concatenate([-turn(part[3], ky), part[4]]))

    sums_all[...] = stacked(far[...], *low, groups * wide)
    slopes_all[...] = stacked(far[:, : 2 * span], *high, groups * wide)
    for g in range(groups):
        here = slice(g * wide, (g + 1) * wide)
        modulus = length(wave_x, ky, g)
        sums = sums_all[here, :] + double(modulus) * slopes_all[here, :]
        for l in range(layers):
            scaled = sums * double(decay(modulus, gain, depth, l, g))
            val[l, g] = stacked(mix[g], *halves(scaled), wide)

    for l in range(layers):

        def strip(i, carry, l=l):
            at = pl.multiple_of(i * STRIP, STRIP)
            pairs = [
                (val[l, g, pl.ds(at, STRIP), :], val[l, g, pl.ds(LANES + at, STRIP), :])
                for g in range(groups)
            ]
            for a, value in enumerate(gather(pairs)):
                here = pl.ds(a * LANES + at, STRIP)
                grids[l][0][here, column], grids[l][1][here, column] = halves(value)
            return carry

        lax.fori_loop(0, LANES // STRIP, strip, 0, unroll=True)


def body(density, observed, active, layer_depth):
    layers, rows, side = density.shape
    period = 2 * side
    tiles = lax.axis_size("tile")
    chips = tiles // 2
    place = lax.axis_index("tile")
    chip, core = place // 2, place % 2
    span = 2 * rows
    groups = side // LANES
    own = groups // 2
    wide = 2 * LANES

    order = ring_order(chips)
    spot = np.argsort(order)
    index = np.zeros((tiles, 2 + 2 * (chips + 1)), np.int32)
    for i in range(tiles):
        p = spot[i // 2]
        index[i, :2] = i % 2, i // 2
        for o in range(chips + 1):
            index[i, 2 + 2 * o] = order[(p - o) % chips]
            index[i, 3 + 2 * o] = order[(p + o) % chips]
    index = lax.dynamic_index_in_dim(jnp.asarray(index), place, 0, False)

    def ring(shift):
        return [
            (2 * int(order[p]) + c, 2 * int(order[(p + shift) % chips]) + c)
            for p in range(chips)
            for c in (0, 1)
        ]

    ahead, back = ring(1), ring(-1)
    pair = [(i, i ^ 1) for i in range(tiles)]

    unit = 2.0 * math.pi / period
    waves = half_waves(side)
    cells = np.arange(side)
    cos_t, sin_t = angle_parts(cells, waves.reshape(-1), period)
    cos_t = cos_t.reshape(side, groups, 1, LANES)
    sin_t = sin_t.reshape(side, groups, 1, LANES)
    full_y = np.concatenate([cos_t, -sin_t], axis=2).reshape(side, 2, side).transpose(1, 2, 0)
    base = np.stack(angle_parts(np.arange(LANES), waves.reshape(-1), period))
    base = jnp.asarray(base, jnp.float32)
    rotate = np.zeros((groups, 16, side))
    rotate[:, 0], rotate[:, 8] = angle_parts(np.arange(groups) * LANES, waves.reshape(-1), period)
    rotate = jnp.asarray(rotate, jnp.float32)
    line = jnp.asarray(np.broadcast_to((waves * unit).reshape(1, -1), (8, side)), jnp.float32)

    low_cells = np.arange(LANES)
    mix = np.zeros((groups, 2 * LANES, 2 * LANES))
    for g in range(groups):
        c, s = angle_parts(waves[g], low_cells, period)
        if g:
            mix[g] = np.block([[c, -s], [s, c]])
        else:
            top = (np.arange(LANES) < LANES // 2)[:, None]
            mix[g] = np.block([[c * top, c * ~top], [s * top, s * ~top]])
    mix_f = table_of(mix, 1)
    mix_b = table_of(mix.transpose(0, 2, 1), 1)

    mix_y = mix.transpose(0, 2, 1) * np.repeat([1.0, -1.0], LANES)
    mix_y = mix_y.reshape(2, own, wide, wide)
    mix_yf = [jnp.asarray(a) for a in np_halves(mix_y)]
    mix_yb = [jnp.asarray(a) for a in np_halves(mix_y.transpose(0, 1, 3, 2))]

    flat_x = (waves * unit).reshape(1, -1, 1)
    flat_y = (waves * unit).reshape(2, 1, -1)
    modulus = np.sqrt(flat_x**2 + flat_y**2).astype(np.float32)
    slab = np.where(modulus > 0, -np.expm1(-modulus) / np.maximum(modulus, 0.001), 1.0)
    twice = np.where(waves == 0, 1.0, 2.0)
    gain = slab * (twice.reshape(1, -1, 1) * twice.reshape(2, 1, -1) / (period * period))
    gain = jnp.asarray(gain, jnp.float32)
    wave_x = jnp.asarray(np.broadcast_to(flat_x[0], (side, LANES)), jnp.float32)
    wave = np.broadcast_to((waves * unit).reshape(2, own, 1, LANES), (2, own, 8, LANES))
    wave = jnp.asarray(wave, jnp.float32)

    far_seen = lax.ppermute(observed, "tile", pair)

    def const(shape):
        return pl.BlockSpec(shape, lambda g, *_: (0,) * len(shape))

    def lanes(shape):
        return pl.BlockSpec(shape, lambda g, *_: (0,) * (len(shape) - 1) + (g,))

    held = pl.BlockSpec(memory_space=pltpu.VMEM)

    def call(kernel, grid, in_specs, out_specs, out_shape, scratch, aliases={}, mib=20):
        return pl.pallas_call(
            kernel,
            grid_spec=pltpu.PrefetchScalarGridSpec(
                num_scalar_prefetch=1,
                grid=(grid,),
                in_specs=in_specs,
                out_specs=out_specs,
                scratch_shapes=scratch,
            ),
            out_shape=out_shape,
            input_output_aliases=aliases,
            compiler_params=pltpu.CompilerParams(
                dimension_semantics=("arbitrary",), vmem_limit_bytes=mib * 1024 * 1024
            ),
        )

    masked = density * active.astype(jnp.float32)[None]
    near, far, gain = call(
        near_kernel,
        1,
        [held] * 4,
        [held] * 3,
        [
            jax.ShapeDtypeStruct((6 * span, period), jnp.bfloat16),
            jax.ShapeDtypeStruct((2 * period, 3 * span), jnp.bfloat16),
            jax.ShapeDtypeStruct((side, side // 2), jnp.float32),
        ],
        [],
        mib=4,
    )(index, base, rotate, line, gain)

    if chips <= 8:
        chains = [masked[0], masked[1]]
        ways = (ahead, back)
        shapes = [jax.ShapeDtypeStruct((side, side), jnp.float32)] * 2
        shapes.append(jax.ShapeDtypeStruct((2 * rows, side), jnp.float32))

        def transformed(step, chains, far, spec):
            args = [index, *chains, *mix_yf]
            kernel, aliases = rows_first, {}
            if step:
                kernel = rows_apart if far is None else rows_next
                kernel = functools.partial(kernel, step)
                args += [*([] if far is None else [far]), *spec]
                aliases = {len(args) - 2: 0, len(args) - 1: 1}
            *spec, give = call(
                kernel,
                1,
                [held] * (len(args) - 1),
                [held] * 3,
                shapes,
                [pltpu.VMEM((groups, 2 * span, wide), jnp.bfloat16)],
                aliases,
                mib=4,
            )(*args)
            return spec, give

        spec = give = other = None
        for step in range(1, chips):
            if step >= 2:
                *chains, give = lax.optimization_barrier((*chains, give))
            came = [lax.ppermute(chains[l], "tile", ways[l]) for l in (0, 1)]
            if step >= 2:
                other = lax.ppermute(give, "tile", pair)
            if step == 4:
                other, near, far, gain, far_seen = lax.optimization_barrier(
                    (other, near, far, gain, far_seen)
                )
            spec, give = transformed(step - 1, chains, other, spec)
            chains = came
        other = lax.ppermute(give, "tile", pair)
        spec, give = transformed(chips - 1, chains, None, spec)
        spec = call(
            functools.partial(rows_last, chips - 1),
            1,
            [held] * 4,
            [held] * 2,
            shapes[:2],
            [],
            {3: 0, 4: 1},
            mib=4,
        )(index, other, lax.ppermute(give, "tile", pair), *spec)
    else:
        whole = lax.all_gather(masked, "tile", axis=1, tiled=True)
        table_y = lax.dynamic_index_in_dim(jnp.asarray(full_y, jnp.float32), core, 0, False)
        spec = lax.dot_general(whole, table_y, (((2,), (1,)), ((), ())), precision=HIGH)
        spec = [spec[0], spec[1]]

    shared = [
        held,
        held,
        pl.BlockSpec((1, 1, 8, LANES), lambda g, p: (p[0], g, 0, 0)),
        held,
    ]
    group_spec = pl.BlockSpec((1, 1, wide, wide), lambda g, p: (p[0], g, 0, 0))
    smem = pl.BlockSpec(memory_space=pltpu.SMEM)
    partial = call(
        forward_kernel,
        own,
        [smem]
        + [held] * 2
        + shared
        + [held]
        + [group_spec] * 2,
        held,
        jax.ShapeDtypeStruct((5 * span, side), jnp.float32),
        [pltpu.VMEM((layers, groups, wide, wide), jnp.bfloat16)] * 2
        + [pltpu.VMEM((period, wide), jnp.bfloat16)] * 4
        + [pltpu.VMEM((own, 5 * span, wide), jnp.float32)],
    )(index, layer_depth, *spec, gain, wave_x, wave, mix_f, near, *mix_yb)

    other = lax.ppermute(partial, "tile", pair)
    predicted, *grids = call(
        adjoint_kernel,
        own,
        [smem]
        + [held] * 4
        + shared
        + [held]
        + [group_spec] * 2,
        [const((6, rows, side))] + [held] * 4,
        [jax.ShapeDtypeStruct((6, rows, side), jnp.float32)]
        + [jax.ShapeDtypeStruct((side, side), jnp.bfloat16)] * 4,
        [
            pltpu.VMEM((5 * span, side), jnp.float32),
            pltpu.VMEM((own, 10 * span, wide), jnp.bfloat16),
            pltpu.VMEM((layers, groups, wide, wide), jnp.float32),
            pltpu.VMEM((period, wide), jnp.float32),
            pltpu.VMEM((period, wide), jnp.float32),
        ],
        mib=26,
    )(
        index, layer_depth, partial, other, observed, far_seen, gain, wave_x, wave,
        mix_b, far, *mix_yf,
    )

    if chips <= 8:

        def share(offset, grids):
            out = call(
                functools.partial(strips_kernel, 2 + 2 * offset),
                1,
                [held] * 6,
                [held] * 3,
                [jax.ShapeDtypeStruct((rows, side), jnp.float32)] * 2
                + [jax.ShapeDtypeStruct((2 * rows, side), jnp.float32)],
                [pltpu.VMEM((own, 2 * span, wide), jnp.float32)],
                mib=4,
            )(index, *grids, *mix_yb)
            return out[:2], lax.ppermute(out[2], "tile", pair)

        def part(ready, l):
            keep, give = ready
            return keep[l] + give[l * rows : (l + 1) * rows]

        ready = share(1, grids)
        now = [part(ready, l) for l in (0, 1)]
        ready = share(2, grids)
        for step in range(1, chips):
            current = ready
            if step < chips - 1:
                now[1], grids = lax.optimization_barrier((now[1], grids))
                ready = share(step + 2, grids)
            now = [lax.ppermute(now[l], "tile", ways[l]) + part(current, l) for l in (0, 1)]
        gradient = jnp.stack(now)
    else:
        table_y = lax.dynamic_index_in_dim(jnp.asarray(full_y, jnp.float32), core, 0, False)
        strip = jnp.stack([h.astype(jnp.float32) + l for h, l in (grids[:2], grids[2:])])
        strip = lax.dot_general(strip, table_y, (((2,), (0,)), ((), ())), precision=HIGH)
        gradient = lax.psum_scatter(strip, "tile", scatter_dimension=1, tiled=True)
    return (predicted, gradient * active.astype(jnp.float32)[None])


def solution(mesh):
    return jax.shard_map(
        body,
        mesh=mesh,
        in_specs=(
            P(None, ("group", "tile"), None),
            P(None, ("group", "tile"), None),
            P(("group", "tile"), None),
            P(),
        ),
        out_specs=(P(None, ("group", "tile"), None), P(None, ("group", "tile"), None)),
        check_vma=False,
    )
```

```python
import functools
import math

import jax
import jax.numpy as jnp
import numpy as np
from jax import lax
from jax.experimental import pallas as pl
from jax.experimental.pallas import tpu as pltpu
from jax.sharding import PartitionSpec as P

LANES = 128
HIGH = lax.Precision.HIGH


def half_waves(side):
    groups = side // LANES
    step = 2 * groups
    even = np.arange(LANES // 2) * step
    rows = [np.concatenate([even, even + groups])]
    for g in range(1, groups):
        rows.append(np.arange(LANES) * step + g)
    index = np.stack(rows)
    return np.where(index < side, index, index - 2 * side)


def angle_parts(left, right, period):
    phase = (left[:, None].astype(np.int64) * right[None, :].astype(np.int64)) % period
    angle = phase * (2.0 * math.pi / period)
    return np.cos(angle), np.sin(angle)


def ring_order(chips):
    width = max(1, int(round(chips ** (1.0 / 3.0))))
    if chips % width:
        width = 1
    height = chips // width
    order = [z * width for z in range(height)]
    for z in reversed(range(height)):
        row = list(range(1, width))
        if (height - 1 - z) % 2:
            row.reverse()
        order += [z * width + x for x in row]
    return np.array(order)


def dot(a, b):
    return jnp.dot(a, b, precision=HIGH)


def halves(a):
    high = a.astype(jnp.bfloat16)
    return high, (a - high.astype(jnp.float32)).astype(jnp.bfloat16)


def np_halves(a):
    a = a.astype(np.float32)
    high = a.astype(jnp.bfloat16)
    return high, (a - high.astype(np.float32)).astype(jnp.bfloat16)


def table_of(a, axis):
    return jnp.asarray(np.concatenate(np_halves(a), axis=axis))


def product(left, right, dims=((1,), (0,))):
    def one(a, b):
        return lax.dot_general(a, b, (dims, ((), ())), preferred_element_type=jnp.float32)

    return one(left[0], right[0]) + (one(left[0], right[1]) + one(left[1], right[0]))


def stacked(table, high, low, rows):
    both = jnp.dot(table, high, preferred_element_type=jnp.float32)
    rest = jnp.dot(table[:rows], low, preferred_element_type=jnp.float32)
    return both[:rows] + (both[rows:] + rest)


def mixed(values, high, low):
    rows = values.shape[0] // 2
    both = jnp.dot(values, high, preferred_element_type=jnp.float32)
    rest = jnp.dot(values[:rows], low, preferred_element_type=jnp.float32)
    return both[:rows] + (both[rows:] + rest)


def accumulate(terms):
    total = None
    for factor, value in terms:
        if abs(factor) < 1e-9:
            continue
        if abs(abs(factor) - 1.0) < 1e-9:
            if total is None:
                total = value if factor > 0 else -value
            else:
                total = total + value if factor > 0 else total - value
        else:
            scaled = value * np.float32(factor)
            total = scaled if total is None else total + scaled
    return total


def spread(f):
    count = len(f)
    half = count // 2
    plus = [f[a] + f[a + half] for a in range(half)]
    minus = [f[a] - f[a + half] for a in range(half)]
    even = [None] + [f[a] + f[count - a] for a in range(1, half)]
    odd = [None] + [f[a] - f[count - a] for a in range(1, half)]
    out = []
    for g in range(count):
        angle = [math.pi * a * g / count for a in range(count)]
        if g == 0:
            top = accumulate([(1.0, plus[a]) for a in range(0, half, 2)])
            low = accumulate([(1.0, plus[a]) for a in range(1, half, 2)])
            out.append((top + low, top - low))
        elif g % 2:
            p = accumulate([(1.0, f[0])] + [(math.cos(angle[a]), odd[a]) for a in range(1, half)])
            q = accumulate(
                [(math.sin(angle[half]), f[half])]
                + [(math.sin(angle[a]), even[a]) for a in range(1, half)]
            )
            out.append((p, q))
        else:
            base = minus if (g // 2) % 2 else plus
            p = accumulate([(math.cos(angle[a]), base[a]) for a in range(half)])
            q = accumulate([(math.sin(angle[a]), base[a]) for a in range(half)])
            out.append((p, q))
    return out


def gather(pairs):
    count = len(pairs)
    half = count // 2
    out = [None] * count
    there = [g for g in range(count) if pairs[g] is not None]

    def wave(a, g):
        angle = math.pi * a * g / count
        return [(math.cos(angle), pairs[g][0]), (math.sin(angle), pairs[g][1])]

    for a in range(half):
        same = []
        if 0 in there:
            same = [(1.0, pairs[0][0]), ((-1.0) ** a, pairs[0][1])]
        for g in there:
            if g and g % 4 == 0:
                same += wave(a, g)
        flip = []
        for g in there:
            if g % 4 == 2:
                flip += wave(a, g)
        same, flip = accumulate(same), accumulate(flip)
        out[a] = same + flip
        out[a + half] = same - flip
    odds = [g for g in there if g % 2]
    for a in range(1, half):
        cosine = accumulate([(math.cos(math.pi * a * g / count), pairs[g][0]) for g in odds])
        sine = accumulate([(math.sin(math.pi * a * g / count), pairs[g][1]) for g in odds])
        out[a] = out[a] + (cosine + sine)
        out[count - a] = out[count - a] + (sine - cosine)
    out[0] = out[0] + accumulate([(1.0, pairs[g][0]) for g in odds])
    out[half] = out[half] + accumulate([(math.sin(math.pi * g / 2), pairs[g][1]) for g in odds])
    return out


def double(a):
    a = jnp.concatenate([a, a], axis=0)
    return jnp.concatenate([a, a], axis=1)


def turn(a, ky):
    return jnp.concatenate([-ky * a[:, LANES:], ky * a[:, :LANES]], axis=1)


def twofold(ky):
    return jnp.concatenate([ky, ky], axis=1)


STRIP = 16


def length(wave_x, ky, g):
    kx = wave_x[g * LANES : (g + 1) * LANES, :]
    return jnp.sqrt(kx * kx + ky * ky)


def decay(modulus, gain, depth, l, g):
    lane = pl.ds(pl.multiple_of(pl.program_id(0) * LANES, LANES), LANES)
    return jnp.exp(-modulus * depth[l]) * gain[g * LANES : (g + 1) * LANES, lane]


def on_core(place, run):
    for c in (0, 1):

        @pl.when(place[0] == c)
        def _(c=c):
            run(c)


def split_lanes(core, own, read, write):
    sums = spread([read(slice(a * LANES, (a + 1) * LANES)) for a in range(2 * own)])
    for g in range(own):
        for k in (0, 1):
            write(g, slice(k * LANES, (k + 1) * LANES), *halves(sums[core * own + g][k]))


def join_lanes(core, own, read):
    pairs = [None] * (2 * own)
    for g in range(own):
        pairs[core * own + g] = (read(g, slice(0, LANES)), read(g, slice(LANES, 2 * LANES)))
    return gather(pairs)


def rows_kernel(at, place, *refs):
    blocks, far, olds, spec, give, val = refs
    core = place[0]
    rows = (far[0][1] if give is None else give).shape[0] // 2
    span = 2 * rows

    def spot(offset, layer, whose):
        chip = place[2 + 2 * offset + layer]
        return pl.ds(pl.multiple_of(chip * span + whose * rows, rows), rows)

    for offset, source in far:
        for l in (0, 1):
            spec[l][spot(offset, l, 1 - core), :] = source[l * rows : (l + 1) * rows, :]
    if not blocks:
        return
    mix_h, mix_l = olds
    own = mix_h.shape[1]
    wide = 2 * LANES
    height = blocks[0].shape[0]
    for n, source in enumerate(blocks):
        for i in range(height // STRIP):
            strip = slice(i * STRIP, (i + 1) * STRIP)
            here = slice(n * height + strip.start, n * height + strip.stop)
            below = slice(span + here.start, span + here.stop)
            f = [source[strip, a * LANES : (a + 1) * LANES] for a in range(2 * own)]
            for g, pair in enumerate(spread(f)):
                for k, value in enumerate(pair):
                    lane = slice(k * LANES, (k + 1) * LANES)
                    val[g, here, lane], val[g, below, lane] = halves(value)
    for g in range(own):
        lane = slice(g * wide, (g + 1) * wide)
        out = mixed(val[core * own + g], mix_h[core, g], mix_l[core, g])
        for l in (0, 1):
            spec[l][spot(at, l, core), lane] = out[l * rows : (l + 1) * rows]
        peer = 1 - core
        give[:, lane] = mixed(val[peer * own + g], mix_h[peer, g], mix_l[peer, g])


def rows_first(place, a, b, mix_h, mix_l, spec_a, spec_b, give, val):
    rows_kernel(0, place, (a, b), (), (mix_h, mix_l), (spec_a, spec_b), give, val)


def rows_next(at, place, a, b, mix_h, mix_l, far, x, y, spec_a, spec_b, give, val):
    rows_kernel(at, place, (a, b), ((at - 1, far),), (mix_h, mix_l), (spec_a, spec_b), give, val)


def rows_apart(at, place, a, b, mix_h, mix_l, x, y, spec_a, spec_b, give, val):
    rows_kernel(at, place, (a, b), (), (mix_h, mix_l), (spec_a, spec_b), give, val)


def rows_last(at, place, before, far, x, y, spec_a, spec_b):
    rows_kernel(
        at, place, (), ((at - 1, before), (at, far)), None, (spec_a, spec_b), None, None
    )


def strips_kernel(at, place, high_a, low_a, high_b, low_b, mix_h, mix_l, *rest):
    keep, give, val = rest[:2], rest[2], rest[3]
    rows = keep[0].shape[0]
    own = mix_h.shape[1]
    span = 2 * rows
    spot = [pl.ds(pl.multiple_of(place[at + l] * span, span), span) for l in (0, 1)]
    for g in range(own):
        lanes = slice(g * 2 * LANES, (g + 1) * 2 * LANES)
        parts = ((high_a, 0), (high_b, 1), (low_a, 0), (low_b, 1))
        values = jnp.concatenate([a[spot[l], lanes] for a, l in parts])
        val[g] = mixed(values, mix_h[place[0], g], mix_l[place[0], g])

    def run(core):
        for l in (0, 1):
            for target, part, base in ((keep[l], core, 0), (give, 1 - core, l * rows)):
                for i in range(rows // 8):
                    start = l * span + part * rows + i * 8
                    blocks = join_lanes(
                        core, own, lambda g, lane: val[g, start : start + 8, lane]
                    )
                    here = slice(base + i * 8, base + (i + 1) * 8)
                    for a, value in enumerate(blocks):
                        target[here, a * LANES : (a + 1) * LANES] = value

    on_core(place, run)


def forward_kernel(
    place, depth, spec_a, spec_b, gain, wave_x, wave, mix, near, back_h, back_l,
    out, val_h, val_l, sum_h, sum_l, steep_h, steep_l, lines,
):
    specs = (spec_a, spec_b)
    layers = len(specs)
    groups = mix.shape[0]
    span = near.shape[0] // 6
    wide = 2 * LANES
    own = groups // 2
    step = pl.program_id(0)
    column = pl.ds(pl.multiple_of(step * wide, wide), wide)

    for l in range(layers):

        def strip(i, carry, l=l):
            at = pl.multiple_of(i * STRIP, STRIP)
            f = [specs[l][pl.ds(a * LANES + at, STRIP), column] for a in range(groups)]
            for g, (p, q) in enumerate(spread(f)):
                high, low = halves(p)
                val_h[l, g, pl.ds(at, STRIP), :] = high
                val_l[l, g, pl.ds(at, STRIP), :] = low
                high, low = halves(q)
                val_h[l, g, pl.ds(LANES + at, STRIP), :] = high
                val_l[l, g, pl.ds(LANES + at, STRIP), :] = low
            return carry

        lax.fori_loop(0, LANES // STRIP, strip, 0, unroll=True)

    ky = wave[0, 0, 0:1, :]
    for g in range(groups):
        total = None
        modulus = length(wave_x, ky, g)
        for l in range(layers):
            cols = stacked(mix[g], val_h[l, g], val_l[l, g], wide)
            cols = cols * double(decay(modulus, gain, depth, l, g))
            total = cols if total is None else total + cols
        here = pl.ds(g * wide, wide)
        sum_h[here, :], sum_l[here, :] = halves(total)
        steep = total * double(modulus)
        steep_h[here, :], steep_l[here, :] = halves(steep)

    plain = stacked(near[...], sum_h[...], sum_l[...], 3 * span)
    slopes = jnp.concatenate([near[: 2 * span], near[3 * span : 5 * span]])
    sloped = stacked(slopes, steep_h[...], steep_l[...], 2 * span)
    both = twofold(ky)
    values = jnp.concatenate(
        [
            plain[2 * span :],
            turn(plain[span : 2 * span], ky),
            sloped[span:],
            -(both * both) * plain[:span],
            turn(sloped[:span], ky),
        ]
    )
    lines[step] = mixed(jnp.concatenate(halves(values)), back_h[0, 0], back_l[0, 0])

    @pl.when(step == own - 1)
    def _():
        def run(core):
            def strip(i, carry):
                here = pl.ds(pl.multiple_of(i * 8, 8), 8)
                blocks = join_lanes(core, own, lambda g, lane: lines[g, here, lane])
                for a, value in enumerate(blocks):
                    out[here, a * LANES : (a + 1) * LANES] = value
                return carry

            lax.fori_loop(0, 5 * span // 8, strip, 0)

        on_core(place, run)


def near_kernel(place, base, rotate, wave, gains, near, far, gain):
    span = near.shape[0] // 6
    start = place[1] * span
    first = pl.multiple_of(lax.rem(start, LANES), STRIP)
    rows = pl.ds(first, span)
    block = lax.div(start, LANES)
    groups = rotate.shape[0]
    gain[...] = gains[place[0]]
    for g in range(groups):
        lane = slice(g * LANES, (g + 1) * LANES)
        both = slice(2 * g * LANES, 2 * (g + 1) * LANES)
        cos_b, sin_b = base[0, rows, lane], base[1, rows, lane]
        cos_a, sin_a = rotate[block, 0:1, lane], rotate[block, 8:9, lane]
        c = cos_b * cos_a - sin_b * sin_a
        s = sin_b * cos_a + cos_b * sin_a
        k = wave[0:1, lane]
        value = jnp.concatenate([c, s], axis=1)
        slope = jnp.concatenate([-k * s, k * c], axis=1)
        bend = -twofold(k * k) * value
        turned = []
        for n, half in enumerate(halves(jnp.concatenate([value, slope, bend]))):
            near[n * 3 * span : (n + 1) * 3 * span, both] = half
            turned.append(half.T)
        high, low = turned
        cut = slice(0, 2 * span), slice(2 * span, 3 * span)
        far[both, :] = jnp.concatenate(
            [part[:, c] for c in cut for part in (high, high, low)], axis=1
        )


def adjoint_kernel(
    place, depth, field, other, seen, far_seen, gain, wave_x, wave, mix, far, fold_h, fold_l,
    predicted, high_a, low_a, high_b, low_b, left, val_y, val, sums_all, slopes_all,
):
    grids = ((high_a, low_a), (high_b, low_b))
    layers = len(grids)
    groups = mix.shape[0]
    rows = predicted.shape[1]
    span = 2 * rows
    wide = 2 * LANES
    own = groups // 2

    @pl.when(pl.program_id(0) == 0)
    def _():
        def total(c, at):
            here = pl.ds(c * span + at, 8)
            return field[here, :] + other[here, :]

        def strip(start, look, write):
            def one(i, carry):
                to = pl.multiple_of(i * 8, 8)
                at = pl.multiple_of(start + i * 8, 8)
                xx, xy, xz, yy, yz = [total(c, at) for c in range(5)]
                zz = -(xx + yy)
                rest_zz = zz - look[5, pl.ds(to, 8), :]
                rest = [
                    rest_zz - (yy - look[3, pl.ds(to, 8), :]),
                    xy - look[1, pl.ds(to, 8), :],
                    rest_zz - (xx - look[0, pl.ds(to, 8), :]),
                    yz - look[4, pl.ds(to, 8), :],
                    xz - look[2, pl.ds(to, 8), :],
                ]
                for c, value in enumerate(rest):
                    left[pl.ds(c * span + at, 8), :] = value
                if write:
                    for c, value in enumerate([xx, xy, xz, yy, yz, zz]):
                        predicted[c, pl.ds(to, 8), :] = value
                return carry

            lax.fori_loop(0, rows // 8, one, 0)

        strip(place[0] * rows, seen, True)
        strip((1 - place[0]) * rows, far_seen, False)

        def run(core):
            def cut(i, carry):
                at = pl.multiple_of(i * STRIP, STRIP)
                here = pl.ds(at, STRIP)
                below = pl.ds(5 * span + at, STRIP)

                def write(g, lane, high, low):
                    val_y[g, here, lane] = high
                    val_y[g, below, lane] = low

                split_lanes(core, own, lambda lane: left[here, lane], write)
                return carry

            lax.fori_loop(0, 5 * span // STRIP, cut, 0)

        on_core(place, run)

    column = pl.ds(pl.multiple_of(pl.program_id(0) * wide, wide), wide)
    back = mixed(val_y[pl.program_id(0)], fold_h[0, 0], fold_l[0, 0])
    ky = wave[0, 0, 0:1, :]
    both = twofold(ky)
    part = [back[c * span : (c + 1) * span] for c in range(5)]
    low = halves(jnp.concatenate([both * both * part[0], -turn(part[1], ky), -part[2]]))
    high = halves(jnp.concatenate([-turn(part[3], ky), part[4]]))

    cut = slice(0, 2 * span), slice(2 * span, 3 * span)
    low = [low[n][c] for c in cut for n in (0, 1, 0)]
    sums_all[...] = jnp.dot(
        far[...], jnp.concatenate(low), preferred_element_type=jnp.float32
    )
    slopes_all[...] = jnp.dot(
        far[:, : 6 * span],
        jnp.concatenate([high[0], high[1], high[0]]),
        preferred_element_type=jnp.float32,
    )
    for g in range(groups):
        here = slice(g * wide, (g + 1) * wide)
        modulus = length(wave_x, ky, g)
        sums = sums_all[here, :] + double(modulus) * slopes_all[here, :]
        for l in range(layers):
            scaled = sums * double(decay(modulus, gain, depth, l, g))
            val[l, g] = stacked(mix[g], *halves(scaled), wide)

    for l in range(layers):

        def strip(i, carry, l=l):
            at = pl.multiple_of(i * STRIP, STRIP)
            pairs = [
                (val[l, g, pl.ds(at, STRIP), :], val[l, g, pl.ds(LANES + at, STRIP), :])
                for g in range(groups)
            ]
            for a, value in enumerate(gather(pairs)):
                here = pl.ds(a * LANES + at, STRIP)
                grids[l][0][here, column], grids[l][1][here, column] = halves(value)
            return carry

        lax.fori_loop(0, LANES // STRIP, strip, 0, unroll=True)


def body(density, observed, active, layer_depth):
    layers, rows, side = density.shape
    period = 2 * side
    tiles = lax.axis_size("tile")
    chips = tiles // 2
    place = lax.axis_index("tile")
    chip, core = place // 2, place % 2
    span = 2 * rows
    groups = side // LANES
    own = groups // 2
    wide = 2 * LANES

    order = ring_order(chips)
    spot = np.argsort(order)
    index = np.zeros((tiles, 2 + 2 * (chips + 1)), np.int32)
    for i in range(tiles):
        p = spot[i // 2]
        index[i, :2] = i % 2, i // 2
        for o in range(chips + 1):
            index[i, 2 + 2 * o] = order[(p - o) % chips]
            index[i, 3 + 2 * o] = order[(p + o) % chips]
    index = lax.dynamic_index_in_dim(jnp.asarray(index), place, 0, False)

    def ring(shift):
        return [
            (2 * int(order[p]) + c, 2 * int(order[(p + shift) % chips]) + c)
            for p in range(chips)
            for c in (0, 1)
        ]

    ahead, back = ring(1), ring(-1)
    pair = [(i, i ^ 1) for i in range(tiles)]

    unit = 2.0 * math.pi / period
    waves = half_waves(side)
    cells = np.arange(side)
    cos_t, sin_t = angle_parts(cells, waves.reshape(-1), period)
    cos_t = cos_t.reshape(side, groups, 1, LANES)
    sin_t = sin_t.reshape(side, groups, 1, LANES)
    full_y = np.concatenate([cos_t, -sin_t], axis=2).reshape(side, 2, side).transpose(1, 2, 0)
    base = np.stack(angle_parts(np.arange(LANES), waves.reshape(-1), period))
    base = jnp.asarray(base, jnp.float32)
    rotate = np.zeros((groups, 16, side))
    rotate[:, 0], rotate[:, 8] = angle_parts(np.arange(groups) * LANES, waves.reshape(-1), period)
    rotate = jnp.asarray(rotate, jnp.float32)
    line = jnp.asarray(np.broadcast_to((waves * unit).reshape(1, -1), (8, side)), jnp.float32)

    low_cells = np.arange(LANES)
    mix = np.zeros((groups, 2 * LANES, 2 * LANES))
    for g in range(groups):
        c, s = angle_parts(waves[g], low_cells, period)
        if g:
            mix[g] = np.block([[c, -s], [s, c]])
        else:
            top = (np.arange(LANES) < LANES // 2)[:, None]
            mix[g] = np.block([[c * top, c * ~top], [s * top, s * ~top]])
    mix_f = table_of(mix, 1)
    mix_b = table_of(mix.transpose(0, 2, 1), 1)

    mix_y = mix.transpose(0, 2, 1) * np.repeat([1.0, -1.0], LANES)
    mix_y = mix_y.reshape(2, own, wide, wide)
    mix_yf = [jnp.asarray(a) for a in np_halves(mix_y)]
    mix_yb = [jnp.asarray(a) for a in np_halves(mix_y.transpose(0, 1, 3, 2))]

    flat_x = (waves * unit).reshape(1, -1, 1)
    flat_y = (waves * unit).reshape(2, 1, -1)
    modulus = np.sqrt(flat_x**2 + flat_y**2).astype(np.float32)
    slab = np.where(modulus > 0, -np.expm1(-modulus) / np.maximum(modulus, 0.001), 1.0)
    twice = np.where(waves == 0, 1.0, 2.0)
    gain = slab * (twice.reshape(1, -1, 1) * twice.reshape(2, 1, -1) / (period * period))
    gain = jnp.asarray(gain, jnp.float32)
    wave_x = jnp.asarray(np.broadcast_to(flat_x[0], (side, LANES)), jnp.float32)
    wave = np.broadcast_to((waves * unit).reshape(2, own, 1, LANES), (2, own, 8, LANES))
    wave = jnp.asarray(wave, jnp.float32)

    far_seen = lax.ppermute(observed, "tile", pair)

    def const(shape):
        return pl.BlockSpec(shape, lambda g, *_: (0,) * len(shape))

    def lanes(shape):
        return pl.BlockSpec(shape, lambda g, *_: (0,) * (len(shape) - 1) + (g,))

    held = pl.BlockSpec(memory_space=pltpu.VMEM)

    def call(kernel, grid, in_specs, out_specs, out_shape, scratch, aliases={}, mib=20):
        return pl.pallas_call(
            kernel,
            grid_spec=pltpu.PrefetchScalarGridSpec(
                num_scalar_prefetch=1,
                grid=(grid,),
                in_specs=in_specs,
                out_specs=out_specs,
                scratch_shapes=scratch,
            ),
            out_shape=out_shape,
            input_output_aliases=aliases,
            compiler_params=pltpu.CompilerParams(
                dimension_semantics=("arbitrary",), vmem_limit_bytes=mib * 1024 * 1024
            ),
        )

    masked = jnp.where(active[None] != 0, density, 0.0)
    near, far, gain = call(
        near_kernel,
        1,
        [held] * 4,
        [held] * 3,
        [
            jax.ShapeDtypeStruct((6 * span, period), jnp.bfloat16),
            jax.ShapeDtypeStruct((period, 9 * span), jnp.bfloat16),
            jax.ShapeDtypeStruct((side, side // 2), jnp.float32),
        ],
        [],
        mib=4,
    )(index, base, rotate, line, gain)

    if chips <= 8:
        chains = [masked[0], masked[1]]
        ways = (ahead, back)
        shapes = [jax.ShapeDtypeStruct((side, side), jnp.float32)] * 2
        shapes.append(jax.ShapeDtypeStruct((2 * rows, side), jnp.float32))

        def transformed(step, chains, far, spec):
            args = [index, *chains, *mix_yf]
            kernel, aliases = rows_first, {}
            if step:
                kernel = rows_apart if far is None else rows_next
                kernel = functools.partial(kernel, step)
                args += [*([] if far is None else [far]), *spec]
                aliases = {len(args) - 2: 0, len(args) - 1: 1}
            *spec, give = call(
                kernel,
                1,
                [held] * (len(args) - 1),
                [held] * 3,
                shapes,
                [pltpu.VMEM((groups, 2 * span, wide), jnp.bfloat16)],
                aliases,
                mib=4,
            )(*args)
            return spec, give

        spec = give = other = None
        for step in range(1, chips):
            if step >= 2:
                *chains, give = lax.optimization_barrier((*chains, give))
            came = [lax.ppermute(chains[l], "tile", ways[l]) for l in (0, 1)]
            if step >= 2:
                other = lax.ppermute(give, "tile", pair)
            if step == 4:
                other, near, far, gain, far_seen = lax.optimization_barrier(
                    (other, near, far, gain, far_seen)
                )
            spec, give = transformed(step - 1, chains, other, spec)
            chains = came
        other = lax.ppermute(give, "tile", pair)
        spec, give = transformed(chips - 1, chains, None, spec)
        spec = call(
            functools.partial(rows_last, chips - 1),
            1,
            [held] * 4,
            [held] * 2,
            shapes[:2],
            [],
            {3: 0, 4: 1},
            mib=4,
        )(index, other, lax.ppermute(give, "tile", pair), *spec)
    else:
        whole = lax.all_gather(masked, "tile", axis=1, tiled=True)
        table_y = lax.dynamic_index_in_dim(jnp.asarray(full_y, jnp.float32), core, 0, False)
        spec = lax.dot_general(whole, table_y, (((2,), (1,)), ((), ())), precision=HIGH)
        spec = [spec[0], spec[1]]

    shared = [
        held,
        held,
        pl.BlockSpec((1, 1, 8, LANES), lambda g, p: (p[0], g, 0, 0)),
        held,
    ]
    group_spec = pl.BlockSpec((1, 1, wide, wide), lambda g, p: (p[0], g, 0, 0))
    smem = pl.BlockSpec(memory_space=pltpu.SMEM)
    partial = call(
        forward_kernel,
        own,
        [smem]
        + [held] * 2
        + shared
        + [held]
        + [group_spec] * 2,
        held,
        jax.ShapeDtypeStruct((5 * span, side), jnp.float32),
        [pltpu.VMEM((layers, groups, wide, wide), jnp.bfloat16)] * 2
        + [pltpu.VMEM((period, wide), jnp.bfloat16)] * 4
        + [pltpu.VMEM((own, 5 * span, wide), jnp.float32)],
    )(index, layer_depth, *spec, gain, wave_x, wave, mix_f, near, *mix_yb)

    other = lax.ppermute(partial, "tile", pair)
    predicted, *grids = call(
        adjoint_kernel,
        own,
        [smem]
        + [held] * 4
        + shared
        + [held]
        + [group_spec] * 2,
        [const((6, rows, side))] + [held] * 4,
        [jax.ShapeDtypeStruct((6, rows, side), jnp.float32)]
        + [jax.ShapeDtypeStruct((side, side), jnp.bfloat16)] * 4,
        [
            pltpu.VMEM((5 * span, side), jnp.float32),
            pltpu.VMEM((own, 10 * span, wide), jnp.bfloat16),
            pltpu.VMEM((layers, groups, wide, wide), jnp.float32),
            pltpu.VMEM((period, wide), jnp.float32),
            pltpu.VMEM((period, wide), jnp.float32),
        ],
        mib=26,
    )(
        index, layer_depth, partial, other, observed, far_seen, gain, wave_x, wave,
        mix_b, far, *mix_yf,
    )

    if chips <= 8:

        def share(offset, grids):
            out = call(
                functools.partial(strips_kernel, 2 + 2 * offset),
                1,
                [held] * 6,
                [held] * 3,
                [jax.ShapeDtypeStruct((rows, side), jnp.float32)] * 2
                + [jax.ShapeDtypeStruct((2 * rows, side), jnp.float32)],
                [pltpu.VMEM((own, 2 * span, wide), jnp.float32)],
                mib=4,
            )(index, *grids, *mix_yb)
            return out[:2], lax.ppermute(out[2], "tile", pair)

        def part(ready, l):
            keep, give = ready
            return keep[l] + give[l * rows : (l + 1) * rows]

        ready = share(1, grids)
        now = [part(ready, l) for l in (0, 1)]
        for step in range(1, chips):
            if step < chips - 1:
                now[1], grids = lax.optimization_barrier((now[1], grids))
            if step == 1:
                ready = share(2, grids)
            current = ready
            if step < chips - 1:
                ready = share(step + 2, grids)
            now = [lax.ppermute(now[l], "tile", ways[l]) + part(current, l) for l in (0, 1)]
        gradient = jnp.stack(now)
    else:
        table_y = lax.dynamic_index_in_dim(jnp.asarray(full_y, jnp.float32), core, 0, False)
        strip = jnp.stack([h.astype(jnp.float32) + l for h, l in (grids[:2], grids[2:])])
        strip = lax.dot_general(strip, table_y, (((2,), (0,)), ((), ())), precision=HIGH)
        gradient = lax.psum_scatter(strip, "tile", scatter_dimension=1, tiled=True)
    return (predicted, gradient * active.astype(jnp.float32)[None])


def solution(mesh):
    return jax.shard_map(
        body,
        mesh=mesh,
        in_specs=(
            P(None, ("group", "tile"), None),
            P(None, ("group", "tile"), None),
            P(("group", "tile"), None),
            P(),
        ),
        out_specs=(P(None, ("group", "tile"), None), P(None, ("group", "tile"), None)),
        check_vma=False,
    )
```
